256 devices in a mesh: inner: 32 (over z, y), outer: 4 (over x_hi, core), head: 2 (over x_lo).
Axes of the slice: x: 4 (x_hi: 2, x_lo: 2; x = x_hi * 2 + x_lo), y: 4, z: 8, core: 2. Of those that a mesh axis runs over, the one named last changes fastest.
Arguments:
- queries: bfloat16 [2, 49152, 2, 4, 128], P(None, ('inner', 'outer'), 'head'), may hold values from -5 to 5
- grad_out: bfloat16 [2, 49152, 2, 4, 128], P(None, ('inner', 'outer'), 'head'), may hold values from -6 to 6
- keys_values: bfloat16 [49152, 2, 2, 128], P(('inner', 'outer'), 'head'), may hold values from -5 to 5
- inputs: bfloat16 [49152, 4096], P(('inner', 'outer')), may hold values from -24 to 24
- kv_weight: bfloat16 [4096, 2, 2, 128], P(None, 'head'), may hold values from -0.09375 to 0.09375
- block_order: int32 [128], replicated, may hold values from 0 to 127, each once
Outputs:
- query_grads: bfloat16 [2, 49152, 2, 4, 128], P(None, ('inner', 'outer'), 'head')
- input_grads: bfloat16 [49152, 4096], P(('inner', 'outer'), 'head')
- weight_grads: float32 [4096, 2, 2, 128], P(('inner', 'outer'), 'head')
The draws below stay inside these ranges and needn't reach their ends.
Inputs may be any that keep to these rules, and one draw needn't show every extreme that they name: `block_order`: each value appears exactly once.
All inputs are finite; a program needn't handle non-finite values.
Results may differ from the reference program's by a relative error of at most 0.015.
Values may be sent and summed in bfloat16 or wider, within the bound.
A program may use at most 128 MiB of HBM per device.

```python
import math
import jax
import jax.numpy as jnp
from jax import lax

D = 4096
HD = 128
QPG = 4
LAYERS = 2
STEPS = 3
TOK_DEV = 384
GROUPS = 2
NBLOCKS = 128
TOKENS = 49152
N_INNER = 32
N_OUTER = 4


def draw_queries(key, part):
    key = jax.random.fold_in(key, 11)
    result = jnp.clip(jax.random.normal(key, (LAYERS, TOKENS, GROUPS, QPG, HD), jnp.float32), -4.5, 4.5)
    return result.astype(jnp.bfloat16)


def draw_keys_values(key, part):
    key = jax.random.fold_in(key, 13)
    result = jnp.clip(jax.random.normal(key, (TOKENS, GROUPS, 2, HD), jnp.float32), -4.5, 4.5)
    return result.astype(jnp.bfloat16)


def spiked(values, key, source, target, shards_of, factor):
    owner, partner = [(jnp.arange(values.shape[position]) // (values.shape[position] // shards_of)).reshape([-1 if axis == position else 1 for axis in range(values.ndim)]) for position in (source, target)]
    chosen = jax.random.permutation(key, shards_of)[partner]
    strong = (owner == chosen) | (owner == (partner + shards_of // 2) % shards_of)
    return jnp.where(strong, factor * values, values)


def levels(rng, dims, shards, least, high):
    def one(position, parts):
        heights = jax.random.uniform(jax.random.fold_in(jax.random.fold_in(rng, 6), position), (parts,), jnp.float32, least / len(shards), high / len(shards))
        return jnp.repeat(jnp.exp(heights), dims[position] // parts).reshape((-1,) + (1,) * (len(dims) - position - 1))

    gain = one(*shards[0])
    for cut in shards[1:]:
        gain = gain * one(*cut)
    return gain


def gaussian(key, extent, width, bound, shards=(), kind=jnp.bfloat16):
    values = width * jax.random.normal(key, extent, jnp.float32)
    if shards:
        values = values * levels(key, extent, shards, -0.22, 0.18)
    return jnp.clip(values, -bound, bound).astype(kind)


def noise_with(key, extent, width, bound, pieces, heavy, kind=jnp.bfloat16):
    drawn = width * jax.random.normal(key, extent, jnp.float32)
    if pieces:
        drawn = drawn * levels(key, extent, pieces, -0.22, 0.18)
    return jnp.clip(spiked(drawn, jax.random.fold_in(key, 3), *heavy), -bound, bound).astype(kind)


def setup_inputs(seed: int = 0) -> dict:
    arg_keys = jax.random.split(jax.random.key(seed), 7)
    return {
        "queries": draw_queries(jax.random.fold_in(arg_keys[6], 71), 0),
        "grad_out": gaussian(arg_keys[1], (LAYERS, TOKENS, GROUPS, QPG, HD), 1.0, 6.0, ((1, 128), (2, 2))),
        "keys_values": draw_keys_values(jax.random.fold_in(arg_keys[6], 71), 0),
        "inputs": noise_with(arg_keys[3], (TOKENS, D), 1.0, 24.0, ((0, 128),), (0, 1, 128, 5.5)),
        "kv_weight": gaussian(arg_keys[4], (D, GROUPS, 2, HD), D ** -0.5, 0.09375, ((1, 2),)),
        "block_order": jax.random.permutation(arg_keys[5], NBLOCKS).astype(jnp.int32),
    }


def block_backward(packed):
    query_rows, grad_rows, key_blocks, query_place, key_places = packed
    score_scale = 1.0 / math.sqrt(HD)
    positions = jnp.arange(TOK_DEV, dtype=jnp.int32)
    query_pos = query_place * TOK_DEV + positions
    key_pos = key_places[:, None] * TOK_DEV + positions[None, :]
    visible = key_pos[None, :, :] <= query_pos[:, None, None]
    queries_wide = query_rows.astype(jnp.float32)
    grads_wide = grad_rows.astype(jnp.float32)
    keys_wide = key_blocks[:, :, 0].astype(jnp.float32)
    values_wide = key_blocks[:, :, 1].astype(jnp.float32)
    scores = jnp.einsum('lqhd,nkd->lhqnk', queries_wide, keys_wide) * score_scale
    scores = jnp.where(visible[None, None], scores, -jnp.inf)
    row_top = lax.optimization_barrier(jnp.max(scores, axis=(3, 4), keepdims=True))
    log_total = row_top + jnp.log(lax.optimization_barrier(jnp.sum(jnp.exp(scores - row_top), axis=(3, 4), keepdims=True)))
    probs_full = jnp.exp(scores - log_total)
    grad_probs = jnp.einsum('lqhd,nkd->lhqnk', grads_wide, values_wide)
    row_delta = lax.optimization_barrier(jnp.sum(probs_full * grad_probs, axis=(3, 4), keepdims=True))
    grad_scores = (probs_full * (grad_probs - row_delta) * score_scale).astype(jnp.bfloat16)
    grad_scores = lax.optimization_barrier(grad_scores).astype(jnp.float32)
    probs_low = lax.optimization_barrier(probs_full.astype(jnp.bfloat16)).astype(jnp.float32)
    query_grad = jnp.einsum('lhqnk,nkd->lqhd', grad_scores, keys_wide)
    key_grad = jnp.einsum('lhqnk,lqhd->nkd', grad_scores, queries_wide)
    value_grad = jnp.einsum('lhqnk,lqhd->nkd', probs_low, grads_wide)
    return (query_grad, jnp.stack([key_grad, value_grad], axis=2))

def reference(queries, grad_out, keys_values, inputs, kv_weight, block_order):
    blocks = N_INNER * N_OUTER
    query_grid = queries.reshape(LAYERS, N_INNER, N_OUTER, TOK_DEV, GROUPS, QPG, HD)
    query_items = jnp.transpose(query_grid, (1, 2, 4, 0, 3, 5, 6)).reshape(blocks * GROUPS, LAYERS, TOK_DEV, QPG, HD)
    grad_grid = grad_out.reshape(LAYERS, N_INNER, N_OUTER, TOK_DEV, GROUPS, QPG, HD)
    grad_items = jnp.transpose(grad_grid, (1, 2, 4, 0, 3, 5, 6)).reshape(blocks * GROUPS, LAYERS, TOK_DEV, QPG, HD)
    pair_grid = keys_values.reshape(N_INNER, N_OUTER, TOK_DEV, GROUPS, 2, HD)
    order_grid = block_order.reshape(N_INNER, N_OUTER)
    gathered = [jnp.roll(pair_grid, distance, axis=0) for distance in range(STEPS)]
    gathered.append(jnp.roll(pair_grid, 1, axis=1))
    key_grid = jnp.stack(gathered, axis=2)
    key_items = jnp.transpose(key_grid, (0, 1, 4, 2, 3, 5, 6)).reshape(blocks * GROUPS, STEPS + 1, TOK_DEV, 2, HD)
    place_list = [jnp.roll(order_grid, distance, axis=0) for distance in range(STEPS)]
    place_list.append(jnp.roll(order_grid, 1, axis=1))
    place_grid = jnp.stack(place_list, axis=2)
    key_places = jnp.repeat(place_grid[:, :, None, :], GROUPS, axis=2).reshape(blocks * GROUPS, STEPS + 1).astype(jnp.int32)
    query_places = jnp.repeat(order_grid[:, :, None], GROUPS, axis=2).reshape(blocks * GROUPS).astype(jnp.int32)
    query_grad, pair_part = lax.map(block_backward, (query_items, grad_items, key_items, query_places, key_places))
    query_grad = query_grad.reshape(N_INNER, N_OUTER, GROUPS, LAYERS, TOK_DEV, QPG, HD)
    query_grads = jnp.transpose(query_grad, (3, 0, 1, 4, 2, 5, 6)).reshape(LAYERS, TOKENS, GROUPS, QPG, HD).astype(jnp.bfloat16)
    pair_part = pair_part.reshape(N_INNER, N_OUTER, GROUPS, STEPS + 1, TOK_DEV, 2, HD)
    summed = jnp.roll(pair_part[:, :, :, STEPS], -1, axis=1)
    for distance in range(STEPS):
        summed = summed + jnp.roll(pair_part[:, :, :, distance], -distance, axis=0)
    pair_grads = jnp.transpose(summed, (0, 1, 3, 2, 4, 5)).reshape(TOKENS, GROUPS, 2, HD)
    pairs_low = pair_grads.astype(jnp.bfloat16)
    input_sum = jnp.zeros((TOKENS, D), jnp.float32)
    for group_index in range(GROUPS):
        group_term = jnp.dot(pairs_low[:, group_index].reshape(TOKENS, 2 * HD), kv_weight[:, group_index].reshape(D, 2 * HD).T, preferred_element_type=jnp.float32)
        group_term = lax.optimization_barrier(group_term.astype(jnp.bfloat16))
        input_sum = input_sum + group_term.astype(jnp.float32)
    input_grads = input_sum.astype(jnp.bfloat16)
    weight_sum = jnp.dot(inputs.T, pairs_low.reshape(TOKENS, GROUPS * 2 * HD), preferred_element_type=jnp.float32)
    weight_grads = (weight_sum / math.sqrt(TOKENS)).reshape(D, GROUPS, 2, HD)
    return (query_grads, input_grads, weight_grads)
```

```python
import functools
import math

import jax
import jax.numpy as jnp
from jax import lax
from jax.experimental import pallas as pl
from jax.experimental.pallas import tpu as pltpu
from jax.sharding import PartitionSpec as P

F32 = jnp.float32
BF16 = jnp.bfloat16
MESH = pl.DeviceIdType.MESH
N_INNER = 32
N_Y = 4
N_Z = 8
N_OUTER = 4
NT = (((1,), (1,)), ((), ()))
TN = (((0,), (0,)), ((), ()))
NN = (((1,), (0,)), ((), ()))
FAR = -1e30
TILE = 512


def dot(a, b, dims):
    return lax.dot_general(a, b, dims, preferred_element_type=F32)


def remote(src, dst, send, recv, **where):
    return pltpu.make_async_remote_copy(
        src_ref=src,
        dst_ref=dst,
        send_sem=send,
        recv_sem=recv,
        device_id=where,
        device_id_type=MESH,
    )


def kernel(
    q, go, kv_raw, order, inputs, weight,
    dq, ig, wg,
    S, DP, top, total, delta, dqt, kv, gout, gin, inp, w_own, w_oth, w_cat,
    pair, pair_t, prod, near, ysend, yfar, relay, yrecv, yacc, zsend, zrecv, fsend, frecv,
    kv_ss, kv_rs, g_ss, g_rs, in_ls, in_ss, in_rs, w_ls, w_ss, w_rs, p_ss, p_rs,
    far_ss, far_rs, y_ss, y_rs, z_ss, z_rs, f_ss, f_rs,
):
    rows = q.shape[0]
    tok = kv.shape[2]
    hd = kv.shape[3]
    group = rows // 2 // tok
    scale = 1.0 / math.sqrt(hd)
    scale2 = scale * math.log2(math.e)
    half_w = w_own.shape[0]
    half_d = half_w // 2
    i = lax.axis_index("inner")
    o = lax.axis_index("outer")
    h = lax.axis_index("head")
    z = i // N_Y
    y = lax.rem(i, N_Y)
    xh = o // 2
    c = lax.rem(o, 2)

    def inner(by):
        return lax.rem(i + by + N_INNER, N_INNER)

    def outer(by):
        return lax.rem(o + by + N_OUTER, N_OUTER)

    def at_z(by):
        return lax.rem(z + by, N_Z) * N_Y + y

    def at_y(place):
        return z * N_Y + place

    core_mate = o + 1 - 2 * c

    barrier = pltpu.get_barrier_semaphore()
    greeted = [{"inner": inner(by)} for by in (1, 2, -1, -2)]
    greeted += [{"outer": outer(by)} for by in (1, 2, 3)]
    greeted += [{"head": 1 - h}]
    greeted += [{"inner": at_y(lax.rem(y + by, N_Y))} for by in (1, 3)]
    greeted += [{"inner": at_z(by)} for by in range(1, N_Z)]
    for where in greeted:
        pl.semaphore_signal(barrier, inc=1, device_id=where, device_id_type=MESH)

    kv[0, 0] = kv_raw[pl.ds(0, tok, 2), :]
    kv[0, 1] = kv_raw[pl.ds(1, tok, 2), :]
    w_local = pltpu.make_async_copy(
        weight.at[pl.ds(pl.multiple_of(h * half_w, half_w), half_w), :], w_own, w_ls
    )
    w_local.start()

    def in_local(zz):
        return pltpu.make_async_copy(
            inputs.at[:, pl.ds(pl.multiple_of(zz * 512 + c * 256, 256), 256)],
            inp.at[zz, pl.ds(0, tok), :],
            in_ls.at[zz],
        )

    def in_remote(zz):
        return remote(
            inputs.at[:, pl.ds(pl.multiple_of(zz * 512 + (1 - c) * 256, 256), 256)],
            inp.at[zz, pl.ds(tok, tok), :],
            in_ss.at[zz],
            in_rs.at[zz],
            outer=core_mate,
        )

    for zz in range(N_Z):
        in_local(zz).start()
    pl.semaphore_wait(barrier, len(greeted))

    forward = [
        remote(kv.at[0], kv.at[1], kv_ss.at[0], kv_rs.at[0], inner=inner(1)),
        remote(kv.at[0], kv.at[2], kv_ss.at[1], kv_rs.at[1], inner=inner(2)),
        remote(kv.at[0], kv.at[3], kv_ss.at[2], kv_rs.at[2], outer=outer(1)),
    ]
    back = [
        remote(gout.at[0], gin.at[0], g_ss.at[0], g_rs.at[0], inner=inner(-1)),
        remote(gout.at[1], gin.at[1], g_ss.at[1], g_rs.at[1], inner=inner(-2)),
        remote(gout.at[2], gin.at[2], g_ss.at[2], g_rs.at[2], outer=outer(-1)),
    ]
    for copy in forward:
        copy.start()
    w_remote = remote(
        weight.at[pl.ds(pl.multiple_of((1 - h) * half_w, half_w), half_w), :],
        w_oth,
        w_ss,
        w_rs,
        head=1 - h,
    )
    w_remote.start()
    for zz in range(N_Z):
        in_remote(zz).start()

    mine = order[i * N_OUTER + o]
    block_ids = [None, inner(-1) * N_OUTER + o, inner(-2) * N_OUTER + o, i * N_OUTER + outer(-1)]
    bias = [jnp.float32(0.0)]
    for block_id in block_ids[1:]:
        bias.append(jnp.where(order[block_id] < mine, 0.0, FAR).astype(F32))

    steps = rows // TILE

    def tile(t):
        return pl.ds(pl.multiple_of(t * TILE, TILE), TILE)

    def look(b):
        def body(t, carry):
            cs = tile(t)
            s = dot(kv[b, 0], q[cs, :], NT)
            if b == 0:
                key = lax.broadcasted_iota(jnp.int32, (tok, TILE), 0)
                row = lax.broadcasted_iota(jnp.int32, (tok, TILE), 1)
                token = (row + lax.rem(t * TILE, rows // 2)) // group
                s = jnp.where(key <= token, s, FAR)
            dp = dot(kv[b, 1], go[cs, :], NT)
            S[b, :, cs] = s
            DP[b, :, cs] = dp
            here = jnp.max(s, axis=0, keepdims=True) * scale2 + bias[b]
            if b == 0:
                e = jnp.exp2(s * scale2 - here)
                top[:, cs] = here
                total[:, cs] = jnp.sum(e, axis=0, keepdims=True)
                delta[:, cs] = jnp.sum(e * dp, axis=0, keepdims=True)
            else:
                old = top[:, cs]
                new = jnp.maximum(old, here)
                factor = jnp.exp2(old - new)
                e = jnp.exp2(s * scale2 - (new - bias[b]))
                top[:, cs] = new
                total[:, cs] = total[:, cs] * factor + jnp.sum(e, axis=0, keepdims=True)
                delta[:, cs] = delta[:, cs] * factor + jnp.sum(e * dp, axis=0, keepdims=True)
            return carry

        lax.fori_loop(0, steps, body, 0, unroll=2)

    def grads(b, first):
        def body(t, carry):
            dk, dv = carry
            cs = tile(t)
            p = jnp.exp2(S[b, :, cs] * scale2 - (top[:, cs] - bias[b]))
            ds = (p * (DP[b, :, cs] - delta[:, cs])).astype(BF16)
            part = dot(kv[b, 0], ds, TN)
            if first:
                dqt[:, cs] = part
            else:
                dqt[:, cs] += part
            return dk + dot(ds, q[cs, :], NN), dv + dot(p.astype(BF16), go[cs, :], NN)

        zero = jnp.zeros((tok, hd), F32)
        return lax.fori_loop(0, steps, body, (zero, zero), unroll=2)

    look(0)
    w_local.wait()
    w_cat[0, :, :hd] = w_own[pl.ds(0, half_d, 2), :]
    w_cat[0, :, hd:] = w_own[pl.ds(1, half_d, 2), :]
    for b in (1, 3, 2):
        forward[b - 1].wait_recv()
        look(b)
    sums = total[...]
    delta[...] = delta[...] / sums
    top[...] = top[...] + jnp.log2(sums)

    for number, b in enumerate((2, 1, 3)):
        dk, dv = grads(b, number == 0)
        gout[b - 1, :, :hd] = (dk * scale).astype(BF16)
        gout[b - 1, :, hd:] = dv.astype(BF16)
        back[b - 1].start()
    dk, dv = grads(0, False)
    dk = dk * scale
    for b in (2, 1, 3):
        back[b - 1].wait_recv()
        dk = dk + gin[b - 1, :, :hd].astype(F32)
        dv = dv + gin[b - 1, :, hd:].astype(F32)
    pair[0, :, :hd] = dk.astype(BF16)
    pair[0, :, hd:] = dv.astype(BF16)
    to_core = remote(pair.at[0], pair.at[1], p_ss.at[0], p_rs.at[0], outer=core_mate)
    to_head = remote(pair.at[0], pair.at[2], p_ss.at[1], p_rs.at[1], head=1 - h)
    to_core.start()
    to_head.start()
    pair_t[:hd, :tok] = dk.T.astype(BF16)
    pair_t[hd:, :tok] = dv.T.astype(BF16)
    to_core.wait_recv()
    pair_t[:, tok:] = pair[1].astype(F32).T.astype(BF16)
    for zz in range(N_Z):
        in_local(zz).wait()
        in_remote(zz).wait_recv()

    j_own = lax.rem(y, 2)
    j_near = 1 - j_own
    owner = y // 2 == c
    not_owner = y // 2 != c
    y_near = 2 * c + j_near
    from_above = lax.rem(y - y_near + N_Y, N_Y) == 1
    side = jnp.where(from_above, 0, 1)

    def z_at(zz):
        return lax.rem(z + 1 + zz, N_Z)

    def relays(zz):
        return (lax.rem(z_at(zz), 2) == 0) == from_above

    def far_copy(zz):
        by = jnp.where(lax.rem(z_at(zz), 2) == 0, N_Y - 1, 1)
        return remote(
            yfar.at[zz], relay.at[zz], far_ss.at[zz], far_rs.at[zz],
            inner=at_y(lax.rem(y + by, N_Y)),
        )

    def near_copy(zz):
        return remote(
            ysend.at[zz], yrecv.at[side, zz], y_ss.at[zz], y_rs.at[side, zz],
            inner=at_y(y_near),
        )

    def z_copy(zz):
        return remote(
            zsend.at[zz], zrecv.at[zz], z_ss.at[zz], z_rs.at[zz], inner=z_at(zz) * N_Y + y
        )

    def produce(zz, carry):
        x = dot(pair_t[...], inp[z_at(zz)], NN)
        prod[0] = x[:, :hd]
        prod[1] = x[:, hd:]

        @pl.when(owner)
        def _():
            yacc[zz] = prod[j_own]

        @pl.when(not_owner)
        def _():
            yfar[zz] = prod[j_own].astype(BF16)
            far_copy(zz).start()

        @pl.when(relays(zz))
        def _():
            near[zz] = prod[j_near]

        @pl.when(jnp.logical_not(relays(zz)))
        def _():
            ysend[zz] = prod[j_near].astype(BF16)
            near_copy(zz).start()

        return carry

    lax.fori_loop(0, N_Z, produce, 0)

    def pass_on(zz, carry):
        @pl.when(relays(zz))
        def _():
            far_copy(zz).wait_recv()
            ysend[zz] = (near[zz] + relay[zz].astype(F32)).astype(BF16)
            near_copy(zz).start()

        return carry

    lax.fori_loop(0, N_Z, pass_on, 0)

    def finish_queries(t, carry):
        cs = tile(t)
        dq[cs, :] = (dqt[:, cs] * scale).T.astype(BF16)
        return carry

    lax.fori_loop(0, steps, finish_queries, 0)
    w_remote.wait_recv()
    w_cat[1, :, :hd] = w_oth[pl.ds(0, half_d, 2), :]
    w_cat[1, :, hd:] = w_oth[pl.ds(1, half_d, 2), :]
    to_head.wait_recv()

    def input_part(t, carry):
        cs = tile(t)
        term = dot(pair[0], w_cat[0, cs, :], NT) + dot(pair[2], w_cat[1, cs, :], NT)
        ig[:, cs] = term.astype(BF16)
        return carry

    lax.fori_loop(0, half_d // TILE, input_part, 0)

    def fin_copy(by):
        place = (core_mate, lax.rem(o + 2, N_OUTER), N_OUTER - 1 - o)[by - 1]
        slot = 0 if by == 1 else 1
        return remote(
            fsend.at[place], frecv.at[slot], f_ss.at[by - 1], f_rs.at[slot], outer=place
        )

    @pl.when(owner)
    def _():
        def gather_y(zz, carry):
            for s in range(2):
                remote(
                    ysend.at[zz], yrecv.at[s, zz], y_ss.at[zz], y_rs.at[s, zz], inner=at_y(y_near)
                ).wait_recv()
            x = yacc[zz] + yrecv[0, zz].astype(F32) + yrecv[1, zz].astype(F32)
            yacc[zz] = x

            @pl.when(zz < N_Z - 1)
            def _():
                zsend[zz] = x.astype(BF16)
                z_copy(zz).start()

            return carry

        lax.fori_loop(0, N_Z, gather_y, 0)

        def gather_z(zz, x):
            z_copy(zz).wait_recv()
            return x + zrecv[zz].astype(F32)

        x = lax.fori_loop(0, N_Z - 1, gather_z, yacc[N_Z - 1])
        x = x.T / math.sqrt(tok * N_INNER * N_OUTER)
        for place in range(N_OUTER):
            fsend[place] = x[place * 32 : place * 32 + 32, :]
        for by in (3, 2, 1):
            fin_copy(by).start()

    @pl.when(owner)
    def _():
        fin_copy(2).wait_recv()
        x = fsend[o] + frecv[1]
        wg[pl.ds(0, 32, 2), :] = x[:, :hd]
        wg[pl.ds(1, 32, 2), :] = x[:, hd:]

    @pl.when(not_owner)
    def _():
        fin_copy(1).wait_recv()
        fin_copy(3).wait_recv()
        x = frecv[0] + frecv[1]
        wg[pl.ds(0, 32, 2), :] = x[:, :hd]
        wg[pl.ds(1, 32, 2), :] = x[:, hd:]

    for copy in forward + back + [w_remote, to_core, to_head]:
        copy.wait_send()

    def sent(zz, carry):
        in_remote(zz).wait_send()
        near_copy(zz).wait_send()

        @pl.when(not_owner)
        def _():
            far_copy(zz).wait_send()

        return carry

    lax.fori_loop(0, N_Z, sent, 0)

    @pl.when(owner)
    def _():
        for zz in range(N_Z - 1):
            z_copy(zz).wait_send()
        for by in (1, 2, 3):
            fin_copy(by).wait_send()


def shards(queries, grad_out, keys_values, inputs, kv_weight, block_order):
    layers, tok, _, per_group, hd = queries.shape
    rows = layers * tok * per_group
    width = inputs.shape[1]
    vmem = pl.BlockSpec(memory_space=pltpu.VMEM)
    smem = pl.BlockSpec(memory_space=pltpu.SMEM)
    hbm = pl.BlockSpec(memory_space=pl.ANY)
    dma = pltpu.SemaphoreType.DMA
    scratch = [
        pltpu.VMEM((4, tok, rows), F32),
        pltpu.VMEM((4, tok, rows), F32),
        pltpu.VMEM((1, rows), F32),
        pltpu.VMEM((1, rows), F32),
        pltpu.VMEM((1, rows), F32),
        pltpu.VMEM((hd, rows), F32),
        pltpu.VMEM((4, 2, tok, hd), BF16),
        pltpu.VMEM((3, tok, 2 * hd), BF16),
        pltpu.VMEM((3, tok, 2 * hd), BF16),
        pltpu.VMEM((N_Z, 2 * tok, 256), BF16),
        pltpu.VMEM((width, hd), BF16),
        pltpu.VMEM((width, hd), BF16),
        pltpu.VMEM((2, width // 2, 2 * hd), BF16),
        pltpu.VMEM((3, tok, 2 * hd), BF16),
        pltpu.VMEM((2 * hd, 2 * tok), BF16),
        pltpu.VMEM((2, 2 * hd, 128), F32),
        pltpu.VMEM((N_Z, 2 * hd, 128), F32),
        pltpu.VMEM((N_Z, 2 * hd, 128), BF16),
        pltpu.VMEM((N_Z, 2 * hd, 128), BF16),
        pltpu.VMEM((N_Z, 2 * hd, 128), BF16),
        pltpu.VMEM((2, N_Z, 2 * hd, 128), BF16),
        pltpu.VMEM((N_Z, 2 * hd, 128), F32),
        pltpu.VMEM((N_Z - 1, 2 * hd, 128), BF16),
        pltpu.VMEM((N_Z - 1, 2 * hd, 128), BF16),
        pltpu.VMEM((N_OUTER, 32, 2 * hd), F32),
        pltpu.VMEM((2, 32, 2 * hd), F32),
        dma((3,)), dma((3,)), dma((3,)), dma((3,)),
        dma((N_Z,)), dma((N_Z,)), dma((N_Z,)), dma, dma, dma, dma((2,)), dma((2,)),
        dma((N_Z,)), dma((N_Z,)), dma((N_Z,)), dma((2, N_Z)),
        dma((N_Z - 1,)), dma((N_Z - 1,)), dma((3,)), dma((2,)),
    ]
    query_out, input_grad, weight_grad = pl.pallas_call(
        kernel,
        out_shape=[
            jax.ShapeDtypeStruct((rows, hd), BF16),
            jax.ShapeDtypeStruct((tok, width // 2), BF16),
            jax.ShapeDtypeStruct((64, hd), F32),
        ],
        in_specs=[vmem, vmem, vmem, smem, hbm, hbm],
        out_specs=[vmem, vmem, vmem],
        scratch_shapes=scratch,
        compiler_params=pltpu.CompilerParams(
            collective_id=0, has_side_effects=True, vmem_limit_bytes=60 * 2**20
        ),
        name="backward",
    )(
        queries.reshape(rows, hd),
        grad_out.reshape(rows, hd),
        keys_values.reshape(tok * 2, hd),
        block_order,
        inputs,
        kv_weight.reshape(width * 2, hd),
    )
    return (
        query_out.reshape(queries.shape),
        input_grad,
        weight_grad.reshape(32, 1, 2, hd),
    )


def solution(mesh):
    return jax.shard_map(
        shards,
        mesh=mesh,
        in_specs=(
            P(None, ("inner", "outer"), "head", None, None),
            P(None, ("inner", "outer"), "head", None, None),
            P(("inner", "outer"), "head", None, None),
            P(("inner", "outer"), None),
            P(None, "head", None, None),
            P(),
        ),
        out_specs=(
            P(None, ("inner", "outer"), "head", None, None),
            P(("inner", "outer"), "head"),
            P(("inner", "outer"), "head", None, None),
        ),
        check_vma=False,
    )
```

```python
import functools
import math

import jax
import jax.numpy as jnp
from jax import lax
from jax.experimental import pallas as pl
from jax.experimental.pallas import tpu as pltpu
from jax.sharding import PartitionSpec as P

F32 = jnp.float32
BF16 = jnp.bfloat16
MESH = pl.DeviceIdType.MESH
N_INNER = 32
N_Y = 4
N_Z = 8
N_OUTER = 4
NT = (((1,), (1,)), ((), ()))
NN = (((1,), (0,)), ((), ()))
FAR = -1e30
TILE = 512


def dot(a, b, dims):
    return lax.dot_general(a, b, dims, preferred_element_type=F32)


def remote(src, dst, send, recv, **where):
    return pltpu.make_async_remote_copy(
        src_ref=src,
        dst_ref=dst,
        send_sem=send,
        recv_sem=recv,
        device_id=where,
        device_id_type=MESH,
    )


def kernel(
    q, go, kv_raw, order, inputs, weight,
    dq, ig, wg,
    E, DP, top, total, delta, fac, k_t, kv, kv_mid, gout, gin, inp, w_own, w_oth, w_cat,
    pair, pair_t, ysend, yrecv, yacc, zsend, zrecv, fsend, frecv,
    kv_ss, kv_rs, g_ss, g_rs, in_ls, in_ss, in_rs, w_ls, w_ss, w_rs, p_ss, p_rs,
    y_ss, y_rs, z_ss, z_rs, f_ss, f_rs,
):
    rows = q.shape[0]
    tok = kv.shape[2]
    hd = kv.shape[3]
    group = rows // 2 // tok
    scale = 1.0 / math.sqrt(hd)
    scale2 = scale * math.log2(math.e)
    half_w = w_own.shape[0]
    half_d = half_w // 2
    steps = rows // TILE
    cut = TILE // group
    i = lax.axis_index("inner")
    o = lax.axis_index("outer")
    h = lax.axis_index("head")
    z = i // N_Y
    y = lax.rem(i, N_Y)
    c = lax.rem(o, 2)

    def inner(by):
        return lax.rem(i + by + N_INNER, N_INNER)

    def outer(by):
        return lax.rem(o + by + N_OUTER, N_OUTER)

    def at_z(by):
        return lax.rem(z + by, N_Z) * N_Y + y

    def at_y(place):
        return z * N_Y + place

    core_mate = o + 1 - 2 * c
    relay_to = lax.rem(at_y(lax.rem(y + 1, N_Y)) + 2, N_INNER)
    two_back = inner(-2)
    relay_from = two_back // N_Y * N_Y + lax.rem(lax.rem(two_back, N_Y) + 3, N_Y)

    barrier = pltpu.get_barrier_semaphore()
    greeted = [{"inner": inner(by)} for by in (1, 2, -1, -2)]
    greeted += [{"outer": outer(by)} for by in (1, 2, 3)]
    greeted += [{"head": 1 - h}, {"inner": relay_to}, {"inner": relay_from}]
    greeted += [{"inner": at_y(lax.rem(y + by, N_Y))} for by in (1, 2, 3)]
    greeted += [{"inner": at_z(by)} for by in range(1, N_Z)]
    for where in greeted:
        pl.semaphore_signal(barrier, inc=1, device_id=where, device_id_type=MESH)

    kv[0, 0] = kv_raw[pl.ds(0, tok, 2), :]
    kv[0, 1] = kv_raw[pl.ds(1, tok, 2), :]
    w_local = pltpu.make_async_copy(
        weight.at[pl.ds(pl.multiple_of(h * half_w, half_w), half_w), :], w_own, w_ls
    )
    w_local.start()

    def in_local(zz):
        return pltpu.make_async_copy(
            inputs.at[:, pl.ds(pl.multiple_of(zz * 512 + c * 256, 256), 256)],
            inp.at[zz, pl.ds(0, tok), :],
            in_ls.at[zz],
        )

    def in_remote(zz):
        return remote(
            inputs.at[:, pl.ds(pl.multiple_of(zz * 512 + (1 - c) * 256, 256), 256)],
            inp.at[zz, pl.ds(tok, tok), :],
            in_ss.at[zz],
            in_rs.at[zz],
            outer=core_mate,
        )

    for zz in range(N_Z):
        in_local(zz).start()
    pl.semaphore_wait(barrier, len(greeted))

    one = remote(kv.at[0], kv.at[1], kv_ss.at[0], kv_rs.at[0], inner=inner(1))
    keys_two = remote(kv.at[0, 0], kv.at[2, 0], kv_ss.at[1], kv_rs.at[1], inner=inner(2))
    values_mid = remote(
        kv.at[0, 1], kv_mid, kv_ss.at[2], kv_rs.at[2], inner=at_y(lax.rem(y + 3, N_Y))
    )
    values_two = remote(kv_mid, kv.at[2, 1], kv_ss.at[3], kv_rs.at[3], inner=relay_to)
    sideways = remote(kv.at[0], kv.at[3], kv_ss.at[4], kv_rs.at[4], outer=outer(1))
    forward = [values_mid, one, sideways, keys_two, values_two]
    for copy in forward[:4]:
        copy.start()

    def back(part, b):
        to = ({"inner": inner(-1)}, {"inner": inner(-2)}, {"outer": outer(-1)})[b - 1]
        at = (part, b - 1)
        return remote(gout.at[at], gin.at[at], g_ss.at[at], g_rs.at[at], **to)

    quarter = pl.ds(pl.multiple_of(c * (half_w // 2), half_w // 2), half_w // 2)
    w_remote = remote(
        weight.at[pl.ds(pl.multiple_of((1 - h) * half_w + c * (half_w // 2), half_w // 2), half_w // 2), :],
        w_oth.at[quarter, :],
        w_ss.at[0],
        w_rs.at[0],
        head=1 - h,
    )
    w_mate = remote(
        w_oth.at[quarter, :], w_oth.at[quarter, :], w_ss.at[1], w_rs.at[1], outer=core_mate
    )
    for zz in range(N_Z):
        in_remote(zz).start()

    mine = order[i * N_OUTER + o]
    block_ids = [None, inner(-1) * N_OUTER + o, inner(-2) * N_OUTER + o, i * N_OUTER + outer(-1)]
    bias = [None]
    for block_id in block_ids[1:]:
        bias.append(jnp.where(order[block_id] < mine, 0.0, FAR).astype(F32))

    def tile(t):
        return pl.ds(pl.multiple_of(t * TILE, TILE), TILE)

    def look_own():
        key = lax.broadcasted_iota(jnp.int32, (cut, TILE), 0)
        row = lax.broadcasted_iota(jnp.int32, (cut, TILE), 1)
        seen = key <= row // group
        for t in range(steps):
            cs = pl.ds(t * TILE, TILE)
            n = (t * cut) % tok + cut
            s = dot(kv[0, 0, :n, :], q[cs, :], NT)
            last = jnp.where(seen, s[n - cut :], FAR)
            s = last if n == cut else jnp.concatenate([s[: n - cut], last], axis=0)
            dp = dot(kv[0, 1, :n, :], go[cs, :], NT)
            here = jnp.max(s, axis=0, keepdims=True) * scale2
            e = jnp.exp2(s * scale2 - here)
            E[0, :n, cs] = e
            DP[0, :n, cs] = dp
            if n < tok:
                E[0, n:, cs] = jnp.zeros((tok - n, TILE), F32)
            top[0, :, cs] = here
            total[:, cs] = jnp.sum(e, axis=0, keepdims=True)
            delta[:, cs] = jnp.sum(e * dp, axis=0, keepdims=True)

    def look(b, before):
        def body(t, carry):
            cs = tile(t)
            s = dot(kv[b, 0], q[cs, :], NT)
            dp = dot(kv[b, 1], go[cs, :], NT)
            old = top[before, :, cs]
            new = jnp.maximum(old, jnp.max(s, axis=0, keepdims=True) * scale2 + bias[b])
            factor = jnp.exp2(old - new)
            e = jnp.exp2(s * scale2 - (new - bias[b]))
            E[b, :, cs] = e
            DP[b, :, cs] = dp
            top[b, :, cs] = new
            total[:, cs] = total[:, cs] * factor + jnp.sum(e, axis=0, keepdims=True)
            delta[:, cs] = delta[:, cs] * factor + jnp.sum(e * dp, axis=0, keepdims=True)
            return carry

        lax.fori_loop(0, steps, body, 0, unroll=2)

    def value_step(b, n, cs):
        p = (E[b, :n, cs] * fac[b, :, cs]).astype(BF16)
        return dot(p, go[cs, :], NN)

    def key_step(b, n, cs):
        ds = E[b, :n, cs] * fac[b, :, cs] * (DP[b, :n, cs] - delta[:, cs])
        E[b, :n, cs] = ds
        return dot(ds.astype(BF16), q[cs, :], NN)

    def block_sum(step, b):
        if b > 0:
            def body(t, total_so_far):
                return total_so_far + step(b, tok, tile(t))

            return lax.fori_loop(0, steps, body, jnp.zeros((tok, hd), F32), unroll=2)
        parts = [None] * (tok // cut)
        for t in range(steps):
            n = (t * cut) % tok + cut
            x = step(0, n, pl.ds(t * TILE, TILE))
            for k in range(n // cut):
                piece = x[k * cut : k * cut + cut]
                parts[k] = piece if parts[k] is None else parts[k] + piece
        return jnp.concatenate(parts, axis=0)

    look_own()
    values_mid.wait_recv()
    values_two.start()
    sideways.wait_recv()
    w_remote.start()
    look(3, 0)
    one.wait_recv()
    look(1, 3)
    keys_two.wait_recv()
    values_two.wait_recv()
    look(2, 1)
    sums = total[...]
    delta[...] = delta[...] / sums
    lse = top[2] + jnp.log2(sums)
    for b in range(4):
        fac[b] = jnp.exp2(top[b] - lse)

    def to_core(part):
        at = (part, 0)
        return remote(pair.at[at], pair.at[part, 1], p_ss.at[at], p_rs.at[at], outer=core_mate)

    def to_head(part):
        at = (part, 1)
        return remote(pair.at[part, 0], pair.at[part, 2], p_ss.at[at], p_rs.at[at], head=1 - h)

    def send_back(part, b, grad):
        gout[part, b - 1] = grad.astype(BF16)
        back(part, b).start()

    def finish_pair(part, grad):
        for b in (2, 1, 3):
            back(part, b).wait_recv()
            grad = grad + gin[part, b - 1].astype(F32)
        pair[part, 0] = grad.astype(BF16)
        to_core(part).start()
        to_head(part).start()
        pair_t[part, :, :tok] = grad.T.astype(BF16)

    owner = y // 2 == c
    not_owner = y // 2 != c

    def z_at(zz):
        return lax.rem(z + 1 + zz, N_Z)

    def above(j):
        return lax.rem(y - (2 * c + j) + N_Y, N_Y)

    def y_copy(part, j, zz):
        return remote(
            ysend.at[part, j, zz],
            yrecv.at[part, above(j) - 1, zz],
            y_ss.at[part, j, zz],
            y_rs.at[part, above(j) - 1, zz],
            inner=at_y(2 * c + j),
        )

    def y_arrival(part, k, zz):
        return remote(
            ysend.at[part, 0, zz], yrecv.at[part, k, zz], y_ss.at[part, 0, zz],
            y_rs.at[part, k, zz], inner=at_y(lax.rem(y + 1, N_Y)),
        )

    def z_copy(part, zz):
        at = (part, zz)
        return remote(
            zsend.at[at], zrecv.at[at], z_ss.at[at], z_rs.at[at], inner=z_at(zz) * N_Y + y
        )

    def produce(part):
        to_core(part).wait_recv()
        pair_t[part, :, tok:] = pair[part, 1].astype(F32).T.astype(BF16)

        def body(zz, carry):
            x = dot(pair_t[part], inp[z_at(zz)], NN)
            for j in range(2):
                piece = x[:, j * hd : j * hd + hd]

                @pl.when(above(j) == 0)
                def _(piece=piece):
                    yacc[part, zz] = piece

                @pl.when(above(j) != 0)
                def _(piece=piece, j=j):
                    ysend[part, j, zz] = piece.astype(BF16)
                    y_copy(part, j, zz).start()

            return carry

        lax.fori_loop(0, N_Z, body, 0, unroll=2)

    def gather_y(part):
        @pl.when(owner)
        def _():
            def body(zz, carry):
                x = yacc[part, zz]
                for k in range(3):
                    y_arrival(part, k, zz).wait_recv()
                    x = x + yrecv[part, k, zz].astype(F32)
                yacc[part, zz] = x

                @pl.when(zz < N_Z - 1)
                def _():
                    zsend[part, zz] = x.astype(BF16)
                    z_copy(part, zz).start()

                return carry

            lax.fori_loop(0, N_Z, body, 0)

    def gather_z(part):
        @pl.when(owner)
        def _():
            def body(zz, x):
                z_copy(part, zz).wait_recv()
                return x + zrecv[part, zz].astype(F32)

            x = lax.fori_loop(0, N_Z - 1, body, yacc[part, N_Z - 1])
            x = x.T / math.sqrt(tok * N_INNER * N_OUTER)
            for place in range(N_OUTER):
                fsend[place, :, part * hd : part * hd + hd] = x[place * 32 : place * 32 + 32, :]

    for b in (2, 1, 3):
        send_back(1, b, block_sum(value_step, b))
    values_own = block_sum(value_step, 0)
    send_back(0, 2, block_sum(key_step, 2) * scale)
    finish_pair(1, values_own)
    w_remote.wait_recv()
    w_mate.start()
    send_back(0, 1, block_sum(key_step, 1) * scale)
    for zz in range(N_Z):
        in_local(zz).wait()
        in_remote(zz).wait_recv()
    produce(1)
    send_back(0, 3, block_sum(key_step, 3) * scale)
    finish_pair(0, block_sum(key_step, 0) * scale)
    gather_y(1)
    produce(0)

    for b in range(4):
        k_t[:, b * tok : b * tok + tok] = kv[b, 0].astype(F32).T.astype(BF16)

    def finish_queries(t, carry):
        cs = tile(t)
        ds = E[:, :, cs].reshape(4 * tok, TILE).astype(BF16)
        dq[cs, :] = (dot(k_t[...], ds, NN) * scale).T.astype(BF16)
        return carry

    lax.fori_loop(0, steps, finish_queries, 0, unroll=2)
    gather_y(0)
    w_local.wait()
    w_mate.wait_recv()
    for k, w in enumerate((w_own, w_oth)):
        w_cat[k, :, :hd] = w[pl.ds(0, half_d, 2), :]
        w_cat[k, :, hd:] = w[pl.ds(1, half_d, 2), :]
    to_head(1).wait_recv()
    to_head(0).wait_recv()

    def input_part(t, carry):
        cs = tile(t)
        term = jnp.zeros((tok, TILE), F32)
        for k, at in enumerate((0, 2)):
            both = jnp.concatenate([pair[0, at], pair[1, at]], axis=1)
            term = term + dot(both, w_cat[k, cs, :], NT)
        ig[:, cs] = term.astype(BF16)
        return carry

    lax.fori_loop(0, half_d // TILE, input_part, 0, unroll=2)
    gather_z(1)
    gather_z(0)

    def fin_copy(by):
        place = (core_mate, lax.rem(o + 2, N_OUTER), N_OUTER - 1 - o)[by - 1]
        slot = 0 if by == 1 else 1
        return remote(
            fsend.at[place], frecv.at[slot], f_ss.at[by - 1], f_rs.at[slot], outer=place
        )

    @pl.when(owner)
    def _():
        for by in (3, 2, 1):
            fin_copy(by).start()
        fin_copy(2).wait_recv()
        x = fsend[o] + frecv[1]
        wg[pl.ds(0, 32, 2), :] = x[:, :hd]
        wg[pl.ds(1, 32, 2), :] = x[:, hd:]

    @pl.when(not_owner)
    def _():
        fin_copy(1).wait_recv()
        fin_copy(3).wait_recv()
        x = frecv[0] + frecv[1]
        wg[pl.ds(0, 32, 2), :] = x[:, :hd]
        wg[pl.ds(1, 32, 2), :] = x[:, hd:]

    for copy in forward + [w_remote, w_mate]:
        copy.wait_send()
    for part in range(2):
        to_core(part).wait_send()
        to_head(part).wait_send()
        for b in (1, 2, 3):
            back(part, b).wait_send()

    def sent(zz, carry):
        in_remote(zz).wait_send()
        for part in range(2):
            for j in range(2):

                @pl.when(above(j) != 0)
                def _(part=part, j=j):
                    y_copy(part, j, zz).wait_send()

        return carry

    lax.fori_loop(0, N_Z, sent, 0)

    @pl.when(owner)
    def _():
        for zz in range(N_Z - 1):
            for part in range(2):
                z_copy(part, zz).wait_send()
        for by in (1, 2, 3):
            fin_copy(by).wait_send()


def shards(queries, grad_out, keys_values, inputs, kv_weight, block_order):
    layers, tok, _, per_group, hd = queries.shape
    rows = layers * tok * per_group
    width = inputs.shape[1]
    vmem = pl.BlockSpec(memory_space=pltpu.VMEM)
    smem = pl.BlockSpec(memory_space=pltpu.SMEM)
    hbm = pl.BlockSpec(memory_space=pl.ANY)
    dma = pltpu.SemaphoreType.DMA
    scratch = [
        pltpu.VMEM((4, tok, rows), F32),
        pltpu.VMEM((4, tok, rows), F32),
        pltpu.VMEM((4, 1, rows), F32),
        pltpu.VMEM((1, rows), F32),
        pltpu.VMEM((1, rows), F32),
        pltpu.VMEM((4, 1, rows), F32),
        pltpu.VMEM((hd, 4 * tok), BF16),
        pltpu.VMEM((4, 2, tok, hd), BF16),
        pltpu.VMEM((tok, hd), BF16),
        pltpu.VMEM((2, 3, tok, hd), BF16),
        pltpu.VMEM((2, 3, tok, hd), BF16),
        pltpu.VMEM((N_Z, 2 * tok, 256), BF16),
        pltpu.VMEM((width, hd), BF16),
        pltpu.VMEM((width, hd), BF16),
        pltpu.VMEM((2, width // 2, 2 * hd), BF16),
        pltpu.VMEM((2, 3, tok, hd), BF16),
        pltpu.VMEM((2, hd, 2 * tok), BF16),
        pltpu.VMEM((2, 2, N_Z, hd, 128), BF16),
        pltpu.VMEM((2, 3, N_Z, hd, 128), BF16),
        pltpu.VMEM((2, N_Z, hd, 128), F32),
        pltpu.VMEM((2, N_Z - 1, hd, 128), BF16),
        pltpu.VMEM((2, N_Z - 1, hd, 128), BF16),
        pltpu.VMEM((N_OUTER, 32, 2 * hd), F32),
        pltpu.VMEM((2, 32, 2 * hd), F32),
        dma((5,)), dma((5,)), dma((2, 3)), dma((2, 3)),
        dma((N_Z,)), dma((N_Z,)), dma((N_Z,)), dma, dma((2,)), dma((2,)), dma((2, 2)), dma((2, 2)),
        dma((2, 2, N_Z)), dma((2, 3, N_Z)),
        dma((2, N_Z - 1)), dma((2, N_Z - 1)), dma((3,)), dma((2,)),
    ]
    query_out, input_grad, weight_grad = pl.pallas_call(
        kernel,
        out_shape=[
            jax.ShapeDtypeStruct((rows, hd), BF16),
            jax.ShapeDtypeStruct((tok, width // 2), BF16),
            jax.ShapeDtypeStruct((64, hd), F32),
        ],
        in_specs=[vmem, vmem, vmem, smem, hbm, hbm],
        out_specs=[vmem, vmem, vmem],
        scratch_shapes=scratch,
        compiler_params=pltpu.CompilerParams(
            collective_id=0, has_side_effects=True, vmem_limit_bytes=60 * 2**20
        ),
        name="backward",
    )(
        queries.reshape(rows, hd),
        grad_out.reshape(rows, hd),
        keys_values.reshape(tok * 2, hd),
        block_order,
        inputs,
        kv_weight.reshape(width * 2, hd),
    )

    def handover(x, y, a, x_out, y_out, a_out, xs, ys, as_, r_sem, w_sem):
        parts = []
        for src, mid, dst, cuts in ((x, xs, x_out, 4), (y, ys, y_out, 4), (a, as_, a_out, 1)):
            n = src.shape[0] // cuts
            for k in range(cuts):
                at = pl.ds(k * n, n)
                parts.append((src.at[at, :], mid.at[at, :], dst.at[at, :]))
        reads = [pltpu.make_async_copy(s, m, r_sem.at[k]) for k, (s, m, _) in enumerate(parts)]
        writes = [pltpu.make_async_copy(m, d, w_sem.at[k]) for k, (_, m, d) in enumerate(parts)]
        for copy in reads:
            copy.start()
        for k, copy in enumerate(writes):
            reads[k].wait()
            copy.start()
        for copy in writes:
            copy.wait()

    query_out, input_grad, weight_grad = pl.pallas_call(
        handover,
        out_shape=[
            jax.ShapeDtypeStruct(query_out.shape, BF16),
            jax.ShapeDtypeStruct(input_grad.shape, BF16),
            jax.ShapeDtypeStruct((64, hd), F32),
        ],
        in_specs=[hbm, hbm, hbm],
        out_specs=[hbm, hbm, hbm],
        scratch_shapes=[
            pltpu.VMEM(query_out.shape, BF16),
            pltpu.VMEM(input_grad.shape, BF16),
            pltpu.VMEM((64, hd), F32),
            dma((9,)),
            dma((9,)),
        ],
        compiler_params=pltpu.CompilerParams(vmem_limit_bytes=60 * 2**20),
        name="handover",
    )(query_out, input_grad, weight_grad)

    return (
        query_out.reshape(queries.shape),
        input_grad,
        weight_grad.reshape(32, 1, 2, hd),
    )


def solution(mesh):
    return jax.shard_map(
        shards,
        mesh=mesh,
        in_specs=(
            P(None, ("inner", "outer"), "head", None, None),
            P(None, ("inner", "outer"), "head", None, None),
            P(("inner", "outer"), "head", None, None),
            P(("inner", "outer"), None),
            P(None, "head", None, None),
            P(),
        ),
        out_specs=(
            P(None, ("inner", "outer"), "head", None, None),
            P(("inner", "outer"), "head"),
            P(("inner", "outer"), "head", None, None),
        ),
        check_vma=False,
    )
```

```python
import functools
import math

import jax
import jax.numpy as jnp
from jax import lax
from jax.experimental import pallas as pl
from jax.experimental.pallas import tpu as pltpu
from jax.sharding import PartitionSpec as P

F32 = jnp.float32
BF16 = jnp.bfloat16
MESH = pl.DeviceIdType.MESH
N_INNER = 32
N_Y = 4
N_Z = 8
N_OUTER = 4
NT = (((1,), (1,)), ((), ()))
NN = (((1,), (0,)), ((), ()))
FAR = -1e30
TILE = 512


def dot(a, b, dims):
    return lax.dot_general(a, b, dims, preferred_element_type=F32)


def remote(src, dst, send, recv, **where):
    return pltpu.make_async_remote_copy(
        src_ref=src,
        dst_ref=dst,
        send_sem=send,
        recv_sem=recv,
        device_id=where,
        device_id_type=MESH,
    )


def kernel(
    q_hbm, go_hbm, kv_raw, order, inputs, weight,
    dq_hbm, ig_hbm, wg,
    q, go, dq, ig,
    E, DP, top, total, delta, fac, k_t, kv, kv_mid, gout, gin, inp, w_own, w_oth, w_cat,
    pair, pair_t, ysend, yrecv, yacc, zsend, zrecv, zacc,
    kv_ss, kv_rs, g_ss, g_rs, in_ls, in_ss, in_rs, w_ls, w_ss, w_rs, p_ss, p_rs,
    y_ss, y_rs, z_ss, z_rs, ready, io_s,
):
    rows = q.shape[0]
    tok = kv.shape[2]
    hd = kv.shape[3]
    group = rows // 2 // tok
    scale = 1.0 / math.sqrt(hd)
    scale2 = scale * math.log2(math.e)
    half_w = w_own.shape[0]
    half_d = half_w // 2
    steps = rows // TILE
    cut = TILE // group
    i = lax.axis_index("inner")
    o = lax.axis_index("outer")
    h = lax.axis_index("head")
    z = i // N_Y
    y = lax.rem(i, N_Y)
    c = lax.rem(o, 2)

    def inner(by):
        return lax.rem(i + by + N_INNER, N_INNER)

    def outer(by):
        return lax.rem(o + by + N_OUTER, N_OUTER)

    def at_z(by):
        return lax.rem(z + by, N_Z) * N_Y + y

    def at_y(place):
        return z * N_Y + place

    core_mate = o + 1 - 2 * c
    relay_to = lax.rem(at_y(lax.rem(y + 1, N_Y)) + 2, N_INNER)
    two_back = inner(-2)
    relay_from = two_back // N_Y * N_Y + lax.rem(lax.rem(two_back, N_Y) + 3, N_Y)

    barrier = pltpu.get_barrier_semaphore()
    greeted = [{"inner": inner(by)} for by in (1, 2, -1, -2)]
    greeted += [{"outer": outer(by)} for by in (1, 2, 3)]
    greeted += [{"head": 1 - h}, {"inner": relay_to}, {"inner": relay_from}]
    greeted += [{"inner": at_y(lax.rem(y + by, N_Y))} for by in (1, 2, 3)]
    greeted += [{"inner": at_z(by)} for by in range(1, N_Z)]
    for where in greeted:
        pl.semaphore_signal(barrier, inc=1, device_id=where, device_id_type=MESH)

    q_in = pltpu.make_async_copy(q_hbm, q, io_s.at[0])
    go_in = pltpu.make_async_copy(go_hbm, go, io_s.at[1])
    dq_out = pltpu.make_async_copy(dq, dq_hbm, io_s.at[2])
    ig_out = pltpu.make_async_copy(ig, ig_hbm, io_s.at[3])
    q_in.start()
    go_in.start()
    kv[0, 0] = kv_raw[pl.ds(0, tok, 2), :]
    kv[0, 1] = kv_raw[pl.ds(1, tok, 2), :]
    w_local = pltpu.make_async_copy(
        weight.at[pl.ds(pl.multiple_of(h * half_w, half_w), half_w), :], w_own, w_ls
    )

    def in_local(zz):
        return pltpu.make_async_copy(
            inputs.at[:, pl.ds(pl.multiple_of(zz * 512 + c * 256, 256), 256)],
            inp.at[zz, pl.ds(0, tok), :],
            in_ls.at[zz],
        )

    def in_remote(zz):
        return remote(
            inputs.at[:, pl.ds(pl.multiple_of(zz * 512 + (1 - c) * 256, 256), 256)],
            inp.at[zz, pl.ds(tok, tok), :],
            in_ss.at[zz],
            in_rs.at[zz],
            outer=core_mate,
        )

    pl.semaphore_wait(barrier, len(greeted))

    one = remote(kv.at[0], kv.at[1], kv_ss.at[0], kv_rs.at[0], inner=inner(1))
    keys_two = remote(kv.at[0, 0], kv.at[2, 0], kv_ss.at[1], kv_rs.at[1], inner=inner(2))
    values_mid = remote(
        kv.at[0, 1], kv_mid, kv_ss.at[2], kv_rs.at[2], inner=at_y(lax.rem(y + 3, N_Y))
    )
    values_two = remote(kv_mid, kv.at[2, 1], kv_ss.at[3], kv_rs.at[3], inner=relay_to)
    sideways = remote(kv.at[0], kv.at[3], kv_ss.at[4], kv_rs.at[4], outer=outer(1))
    forward = [values_mid, one, sideways, keys_two, values_two]
    for copy in forward[:4]:
        copy.start()

    def back(part, b):
        to = ({"inner": inner(-1)}, {"inner": inner(-2)}, {"outer": outer(-1)})[b - 1]
        at = (part, b - 1)
        return remote(gout.at[at], gin.at[at], g_ss.at[at], g_rs.at[at], **to)

    quarter = pl.ds(pl.multiple_of(c * (half_w // 2), half_w // 2), half_w // 2)
    w_remote = remote(
        weight.at[pl.ds(pl.multiple_of((1 - h) * half_w + c * (half_w // 2), half_w // 2), half_w // 2), :],
        w_oth.at[quarter, :],
        w_ss.at[0],
        w_rs.at[0],
        head=1 - h,
    )
    w_mate = remote(
        w_oth.at[quarter, :], w_oth.at[quarter, :], w_ss.at[1], w_rs.at[1], outer=core_mate
    )
    for by in range(1, N_Z):
        pl.semaphore_signal(ready, inc=1, device_id={"inner": at_z(by)}, device_id_type=MESH)
    w_local.start()
    for zz in range(N_Z):
        in_local(zz).start()
        in_remote(zz).start()

    mine = order[i * N_OUTER + o]
    block_ids = [None, inner(-1) * N_OUTER + o, inner(-2) * N_OUTER + o, i * N_OUTER + outer(-1)]
    bias = [None]
    for block_id in block_ids[1:]:
        bias.append(jnp.where(order[block_id] < mine, 0.0, FAR).astype(F32))

    def tile(t):
        return pl.ds(pl.multiple_of(t * TILE, TILE), TILE)

    def look_own():
        key = lax.broadcasted_iota(jnp.int32, (cut, TILE), 0)
        row = lax.broadcasted_iota(jnp.int32, (cut, TILE), 1)
        seen = key <= row // group
        for t in range(steps):
            cs = pl.ds(t * TILE, TILE)
            n = (t * cut) % tok + cut
            s = dot(kv[0, 0, :n, :], q[cs, :], NT)
            last = jnp.where(seen, s[n - cut :], FAR)
            s = last if n == cut else jnp.concatenate([s[: n - cut], last], axis=0)
            dp = dot(kv[0, 1, :n, :], go[cs, :], NT)
            here = jnp.max(s, axis=0, keepdims=True) * scale2
            e = jnp.exp2(s * scale2 - here)
            E[0, :n, cs] = e
            DP[0, :n, cs] = dp
            if n < tok:
                E[0, n:, cs] = jnp.zeros((tok - n, TILE), F32)
            top[0, :, cs] = here
            total[:, cs] = jnp.sum(e, axis=0, keepdims=True)
            delta[:, cs] = jnp.sum(e * dp, axis=0, keepdims=True)

    def look(b, before):
        def body(t, carry):
            cs = tile(t)
            s = dot(kv[b, 0], q[cs, :], NT)
            dp = dot(kv[b, 1], go[cs, :], NT)
            old = top[before, :, cs]
            new = jnp.maximum(old, jnp.max(s, axis=0, keepdims=True) * scale2 + bias[b])
            factor = jnp.exp2(old - new)
            e = jnp.exp2(s * scale2 - (new - bias[b]))
            E[b, :, cs] = e
            DP[b, :, cs] = dp
            top[b, :, cs] = new
            total[:, cs] = total[:, cs] * factor + jnp.sum(e, axis=0, keepdims=True)
            delta[:, cs] = delta[:, cs] * factor + jnp.sum(e * dp, axis=0, keepdims=True)
            return carry

        lax.fori_loop(0, steps, body, 0, unroll=2)

    def value_step(b, n, cs):
        p = (E[b, :n, cs] * fac[b, :, cs]).astype(BF16)
        return dot(p, go[cs, :], NN)

    def key_step(b, n, cs):
        ds = E[b, :n, cs] * fac[b, :, cs] * (DP[b, :n, cs] - delta[:, cs])
        E[b, :n, cs] = ds
        return dot(ds.astype(BF16), q[cs, :], NN)

    def block_sum(step, b):
        if b > 0:
            def body(t, total_so_far):
                return total_so_far + step(b, tok, tile(t))

            return lax.fori_loop(0, steps, body, jnp.zeros((tok, hd), F32), unroll=2)
        parts = [None] * (tok // cut)
        for t in range(steps):
            n = (t * cut) % tok + cut
            x = step(0, n, pl.ds(t * TILE, TILE))
            for k in range(n // cut):
                piece = x[k * cut : k * cut + cut]
                parts[k] = piece if parts[k] is None else parts[k] + piece
        return jnp.concatenate(parts, axis=0)

    q_in.wait()
    go_in.wait()
    look_own()
    values_mid.wait_recv()
    values_two.start()
    sideways.wait_recv()
    w_remote.start()
    look(3, 0)
    one.wait_recv()
    look(1, 3)
    keys_two.wait_recv()
    values_two.wait_recv()
    look(2, 1)
    sums = total[...]
    delta[...] = delta[...] / sums
    lse = top[2] + jnp.log2(sums)
    for b in range(4):
        fac[b] = jnp.exp2(top[b] - lse)

    def to_core(part):
        at = (part, 0)
        return remote(pair.at[at], pair.at[part, 1], p_ss.at[at], p_rs.at[at], outer=core_mate)

    def to_head(part):
        at = (part, 1)
        return remote(pair.at[part, 0], pair.at[part, 2], p_ss.at[at], p_rs.at[at], head=1 - h)

    def send_back(part, b, grad):
        gout[part, b - 1] = grad.astype(BF16)
        back(part, b).start()

    def finish_pair(part, grad):
        for b in (2, 1, 3):
            back(part, b).wait_recv()
            grad = grad + gin[part, b - 1].astype(F32)
        pair[part, 0] = grad.astype(BF16)
        to_core(part).start()
        to_head(part).start()
        pair_t[part, :, :tok] = grad.T.astype(BF16)

    owner = y // 2 == c
    not_owner = y // 2 != c

    def z_at(zz):
        return lax.rem(z + 1 + zz, N_Z)

    def above(j):
        return lax.rem(y - (2 * c + j) + N_Y, N_Y)

    def y_copy(part, j, zz):
        return remote(
            ysend.at[part, j, zz],
            yrecv.at[part, above(j) - 1, zz],
            y_ss.at[part, j, zz],
            y_rs.at[part, above(j) - 1, zz],
            inner=at_y(2 * c + j),
        )

    def y_arrival(part, k, zz):
        return remote(
            ysend.at[part, 0, zz], yrecv.at[part, k, zz], y_ss.at[part, 0, zz],
            y_rs.at[part, k, zz], inner=at_y(lax.rem(y + 1, N_Y)),
        )

    def z_copy(part, zz, place):
        slot = 2 * zz + jnp.where(o // 2 == place // 2, 0, 1)
        return remote(
            zsend.at[part, zz, pl.ds(place * 32, 32), :],
            zrecv.at[part, slot],
            z_ss.at[part, zz, place],
            z_rs.at[part, slot],
            inner=z_at(zz) * N_Y + y,
            outer=place,
        )

    def z_arrival(part, slot):
        return remote(
            zsend.at[part, 0, pl.ds(0, 32), :], zrecv.at[part, slot], z_ss.at[part, 0, 0],
            z_rs.at[part, slot], inner=z_at(0) * N_Y + y,
        )

    def produce(part):
        to_core(part).wait_recv()
        pair_t[part, :, tok:] = pair[part, 1].astype(F32).T.astype(BF16)

        def body(zz, carry):
            x = dot(pair_t[part], inp[z_at(zz)], NN)
            for j in range(2):
                piece = x[:, j * hd : j * hd + hd]

                @pl.when(above(j) == 0)
                def _(piece=piece):
                    yacc[part, zz] = piece

                @pl.when(above(j) != 0)
                def _(piece=piece, j=j):
                    ysend[part, j, zz] = piece.astype(BF16)
                    y_copy(part, j, zz).start()

            return carry

        lax.fori_loop(0, N_Z, body, 0, unroll=2)

    def gather_y(part):
        @pl.when(owner)
        def _():
            def body(zz, carry):
                x = yacc[part, zz]
                for k in range(3):
                    y_arrival(part, k, zz).wait_recv()
                    x = x + yrecv[part, k, zz].astype(F32)
                x = x.T
                zsend[part, zz] = x.astype(BF16)
                for place in range(N_OUTER):

                    @pl.when((zz < N_Z - 1) | (place != o))
                    def _(place=place):
                        z_copy(part, zz, place).start()

                @pl.when(zz == N_Z - 1)
                def _():
                    for place in range(N_OUTER):

                        @pl.when(place == o)
                        def _(place=place):
                            zacc[part] = x[place * 32 : place * 32 + 32, :]

                return carry

            lax.fori_loop(0, N_Z, body, 0)

    def gather_z(part):
        @pl.when(not_owner)
        def _():
            z_arrival(part, 2 * N_Z - 2).wait_recv()
            zacc[part] = zrecv[part, 2 * N_Z - 2].astype(F32)

        def body(slot, x):
            z_arrival(part, slot).wait_recv()
            return x + zrecv[part, slot].astype(F32)

        x = lax.fori_loop(0, 2 * N_Z - 2, body, zacc[part])
        x = body(2 * N_Z - 1, x) / math.sqrt(tok * N_INNER * N_OUTER)
        wg[pl.ds(part, 32, 2), :] = x

    for b in (2, 1, 3):
        send_back(1, b, block_sum(value_step, b))
    values_own = block_sum(value_step, 0)
    send_back(0, 2, block_sum(key_step, 2) * scale)
    finish_pair(1, values_own)
    w_remote.wait_recv()
    w_mate.start()
    send_back(0, 1, block_sum(key_step, 1) * scale)
    for zz in range(N_Z):
        in_local(zz).wait()
        in_remote(zz).wait_recv()
    produce(1)
    send_back(0, 3, block_sum(key_step, 3) * scale)
    finish_pair(0, block_sum(key_step, 0) * scale)
    pl.semaphore_wait(ready, N_Z - 1)
    gather_y(1)
    produce(0)

    for b in range(4):
        k_t[:, b * tok : b * tok + tok] = kv[b, 0].astype(F32).T.astype(BF16)

    def finish_queries(t, carry):
        cs = tile(t)
        ds = E[:, :, cs].reshape(4 * tok, TILE).astype(BF16)
        dq[cs, :] = (dot(k_t[...], ds, NN) * scale).T.astype(BF16)
        return carry

    lax.fori_loop(0, steps, finish_queries, 0, unroll=2)
    dq_out.start()
    gather_y(0)
    w_local.wait()
    w_mate.wait_recv()
    for k, w in enumerate((w_own, w_oth)):
        w_cat[k, :, :hd] = w[pl.ds(0, half_d, 2), :]
        w_cat[k, :, hd:] = w[pl.ds(1, half_d, 2), :]
    to_head(1).wait_recv()
    to_head(0).wait_recv()

    def input_part(t, carry):
        cs = tile(t)
        term = jnp.zeros((tok, TILE), F32)
        for k, at in enumerate((0, 2)):
            both = jnp.concatenate([pair[0, at], pair[1, at]], axis=1)
            term = term + dot(both, w_cat[k, cs, :], NT)
        ig[:, cs] = term.astype(BF16)
        return carry

    lax.fori_loop(0, half_d // TILE, input_part, 0, unroll=2)
    ig_out.start()
    gather_z(1)
    gather_z(0)

    for copy in forward + [w_remote, w_mate]:
        copy.wait_send()
    for part in range(2):
        to_core(part).wait_send()
        to_head(part).wait_send()
        for b in (1, 2, 3):
            back(part, b).wait_send()

    def sent(zz, carry):
        in_remote(zz).wait_send()
        for part in range(2):
            for j in range(2):

                @pl.when(above(j) != 0)
                def _(part=part, j=j):
                    y_copy(part, j, zz).wait_send()

        return carry

    lax.fori_loop(0, N_Z, sent, 0)

    @pl.when(owner)
    def _():
        def sent_z(zz, carry):
            for part in range(2):
                for place in range(N_OUTER):

                    @pl.when((zz < N_Z - 1) | (place != o))
                    def _(part=part, place=place):
                        z_copy(part, zz, place).wait_send()

            return carry

        lax.fori_loop(0, N_Z, sent_z, 0)

    dq_out.wait()
    ig_out.wait()


def shards(queries, grad_out, keys_values, inputs, kv_weight, block_order):
    layers, tok, _, per_group, hd = queries.shape
    rows = layers * tok * per_group
    width = inputs.shape[1]
    vmem = pl.BlockSpec(memory_space=pltpu.VMEM)
    smem = pl.BlockSpec(memory_space=pltpu.SMEM)
    hbm = pl.BlockSpec(memory_space=pl.ANY)
    dma = pltpu.SemaphoreType.DMA
    scratch = [
        pltpu.VMEM((rows, hd), BF16),
        pltpu.VMEM((rows, hd), BF16),
        pltpu.VMEM((rows, hd), BF16),
        pltpu.VMEM((tok, width // 2), BF16),
        pltpu.VMEM((4, tok, rows), F32),
        pltpu.VMEM((4, tok, rows), F32),
        pltpu.VMEM((4, 1, rows), F32),
        pltpu.VMEM((1, rows), F32),
        pltpu.VMEM((1, rows), F32),
        pltpu.VMEM((4, 1, rows), F32),
        pltpu.VMEM((hd, 4 * tok), BF16),
        pltpu.VMEM((4, 2, tok, hd), BF16),
        pltpu.VMEM((tok, hd), BF16),
        pltpu.VMEM((2, 3, tok, hd), BF16),
        pltpu.VMEM((2, 3, tok, hd), BF16),
        pltpu.VMEM((N_Z, 2 * tok, 256), BF16),
        pltpu.VMEM((width, hd), BF16),
        pltpu.VMEM((width, hd), BF16),
        pltpu.VMEM((2, width // 2, 2 * hd), BF16),
        pltpu.VMEM((2, 3, tok, hd), BF16),
        pltpu.VMEM((2, hd, 2 * tok), BF16),
        pltpu.VMEM((2, 2, N_Z, hd, 128), BF16),
        pltpu.VMEM((2, 3, N_Z, hd, 128), BF16),
        pltpu.VMEM((2, N_Z, hd, 128), F32),
        pltpu.VMEM((2, N_Z, 128, hd), BF16),
        pltpu.VMEM((2, 2 * N_Z, 32, hd), BF16),
        pltpu.VMEM((2, 32, hd), F32),
        dma((5,)), dma((5,)), dma((2, 3)), dma((2, 3)),
        dma((N_Z,)), dma((N_Z,)), dma((N_Z,)), dma, dma((2,)), dma((2,)), dma((2, 2)), dma((2, 2)),
        dma((2, 2, N_Z)), dma((2, 3, N_Z)),
        dma((2, N_Z, N_OUTER)), dma((2, 2 * N_Z)), pltpu.SemaphoreType.REGULAR, dma((4,)),
    ]
    query_out, input_grad, weight_grad = pl.pallas_call(
        kernel,
        out_shape=[
            jax.ShapeDtypeStruct((rows, hd), BF16),
            jax.ShapeDtypeStruct((tok, width // 2), BF16),
            jax.ShapeDtypeStruct((64, hd), F32),
        ],
        in_specs=[hbm, hbm, vmem, smem, hbm, hbm],
        out_specs=[hbm, hbm, vmem],
        scratch_shapes=scratch,
        compiler_params=pltpu.CompilerParams(
            collective_id=0, has_side_effects=True, vmem_limit_bytes=60 * 2**20
        ),
        name="backward",
    )(
        queries.reshape(rows, hd),
        grad_out.reshape(rows, hd),
        keys_values.reshape(tok * 2, hd),
        block_order,
        inputs,
        kv_weight.reshape(width * 2, hd),
    )

    def handover(x, y, a, x_out, y_out, a_out, xs, ys, as_, r_sem, w_sem):
        parts = []
        for src, mid, dst, cuts in ((x, xs, x_out, 4), (y, ys, y_out, 4), (a, as_, a_out, 1)):
            n = src.shape[0] // cuts
            for k in range(cuts):
                at = pl.ds(k * n, n)
                parts.append((src.at[at, :], mid.at[at, :], dst.at[at, :]))
        reads = [pltpu.make_async_copy(s, m, r_sem.at[k]) for k, (s, m, _) in enumerate(parts)]
        writes = [pltpu.make_async_copy(m, d, w_sem.at[k]) for k, (_, m, d) in enumerate(parts)]
        for copy in reads:
            copy.start()
        for k, copy in enumerate(writes):
            reads[k].wait()
            copy.start()
        for copy in writes:
            copy.wait()

    query_out, input_grad, weight_grad = pl.pallas_call(
        handover,
        out_shape=[
            jax.ShapeDtypeStruct(query_out.shape, BF16),
            jax.ShapeDtypeStruct(input_grad.shape, BF16),
            jax.ShapeDtypeStruct((64, hd), F32),
        ],
        in_specs=[hbm, hbm, hbm],
        out_specs=[hbm, hbm, hbm],
        scratch_shapes=[
            pltpu.VMEM(query_out.shape, BF16),
            pltpu.VMEM(input_grad.shape, BF16),
            pltpu.VMEM((64, hd), F32),
            dma((9,)),
            dma((9,)),
        ],
        compiler_params=pltpu.CompilerParams(vmem_limit_bytes=60 * 2**20),
        name="handover",
    )(query_out, input_grad, weight_grad)

    return (
        query_out.reshape(queries.shape),
        input_grad,
        weight_grad.reshape(32, 1, 2, hd),
    )


def solution(mesh):
    return jax.shard_map(
        shards,
        mesh=mesh,
        in_specs=(
            P(None, ("inner", "outer"), "head", None, None),
            P(None, ("inner", "outer"), "head", None, None),
            P(("inner", "outer"), "head", None, None),
            P(("inner", "outer"), None),
            P(None, "head", None, None),
            P(),
        ),
        out_specs=(
            P(None, ("inner", "outer"), "head", None, None),
            P(("inner", "outer"), "head"),
            P(("inner", "outer"), "head", None, None),
        ),
        check_vma=False,
    )
```

```python
import functools
import math

import jax
import jax.numpy as jnp
from jax import lax
from jax.experimental import pallas as pl
from jax.experimental.pallas import tpu as pltpu
from jax.sharding import PartitionSpec as P

F32 = jnp.float32
BF16 = jnp.bfloat16
MESH = pl.DeviceIdType.MESH
N_INNER = 32
N_Y = 4
N_Z = 8
N_OUTER = 4
NT = (((1,), (1,)), ((), ()))
NN = (((1,), (0,)), ((), ()))
FAR = -1e30
TILE = 512


def dot(a, b, dims):
    return lax.dot_general(a, b, dims, preferred_element_type=F32)


def remote(src, dst, send, recv, **where):
    return pltpu.make_async_remote_copy(
        src_ref=src,
        dst_ref=dst,
        send_sem=send,
        recv_sem=recv,
        device_id=where,
        device_id_type=MESH,
    )


def kernel(
    q_hbm, go_hbm, kv_raw, order, inputs, weight,
    dq_hbm, ig_hbm, wg,
    q, go, dq, ig,
    E, DP, top, total, delta, fac, k_t, kv, kv_mid, gout, gin, inp, w_own, w_oth, w_cat,
    pair, pair_t, ysend, yrecv, yacc, zsend, zrecv, zacc,
    kv_ss, kv_rs, g_ss, g_rs, in_ls, in_ss, in_rs, w_ls, w_ss, w_rs, p_ss, p_rs,
    y_ss, y_rs, z_ss, z_rs, ready, io_s,
):
    rows = q.shape[0]
    tok = kv.shape[2]
    hd = kv.shape[3]
    group = rows // 2 // tok
    scale = 1.0 / math.sqrt(hd)
    scale2 = scale * math.log2(math.e)
    half_w = w_own.shape[0]
    half_d = half_w // 2
    steps = rows // TILE
    cut = TILE // group
    i = lax.axis_index("inner")
    o = lax.axis_index("outer")
    h = lax.axis_index("head")
    z = i // N_Y
    y = lax.rem(i, N_Y)
    c = lax.rem(o, 2)

    def inner(by):
        return lax.rem(i + by + N_INNER, N_INNER)

    def outer(by):
        return lax.rem(o + by + N_OUTER, N_OUTER)

    def at_z(by):
        return lax.rem(z + by, N_Z) * N_Y + y

    def at_y(place):
        return z * N_Y + place

    core_mate = o + 1 - 2 * c
    relay_to = lax.rem(at_y(lax.rem(y + 1, N_Y)) + 2, N_INNER)
    two_back = inner(-2)
    relay_from = two_back // N_Y * N_Y + lax.rem(lax.rem(two_back, N_Y) + 3, N_Y)

    barrier = pltpu.get_barrier_semaphore()
    greeted = [{"inner": inner(by)} for by in (1, 2, -1, -2)]
    greeted += [{"outer": outer(by)} for by in (1, 2, 3)]
    greeted += [{"head": 1 - h}, {"inner": relay_to}, {"inner": relay_from}]
    greeted += [{"inner": at_y(lax.rem(y + by, N_Y))} for by in (1, 2, 3)]
    greeted += [{"inner": at_z(by)} for by in range(1, N_Z)]
    for where in greeted:
        pl.semaphore_signal(barrier, inc=1, device_id=where, device_id_type=MESH)

    q_in = pltpu.make_async_copy(q_hbm, q, io_s.at[0])
    go_in = pltpu.make_async_copy(go_hbm, go, io_s.at[1])
    dq_out = pltpu.make_async_copy(dq, dq_hbm, io_s.at[2])
    ig_out = pltpu.make_async_copy(ig, ig_hbm, io_s.at[3])
    q_in.start()
    go_in.start()
    kv[0, 0] = kv_raw[pl.ds(0, tok, 2), :]
    kv[0, 1] = kv_raw[pl.ds(1, tok, 2), :]
    w_local = pltpu.make_async_copy(
        weight.at[pl.ds(pl.multiple_of(h * half_w, half_w), half_w), :], w_own, w_ls
    )

    def in_local(zz):
        return pltpu.make_async_copy(
            inputs.at[:, pl.ds(pl.multiple_of(zz * 512 + c * 256, 256), 256)],
            inp.at[zz, pl.ds(0, tok), :],
            in_ls.at[zz],
        )

    def in_remote(zz):
        return remote(
            inputs.at[:, pl.ds(pl.multiple_of(zz * 512 + (1 - c) * 256, 256), 256)],
            inp.at[zz, pl.ds(tok, tok), :],
            in_ss.at[zz],
            in_rs.at[zz],
            outer=core_mate,
        )

    pl.semaphore_wait(barrier, len(greeted))

    one = remote(kv.at[0], kv.at[1], kv_ss.at[0], kv_rs.at[0], inner=inner(1))
    keys_two = remote(kv.at[0, 0], kv.at[2, 0], kv_ss.at[1], kv_rs.at[1], inner=inner(2))
    values_mid = remote(
        kv.at[0, 1], kv_mid, kv_ss.at[2], kv_rs.at[2], inner=at_y(lax.rem(y + 3, N_Y))
    )
    values_two = remote(kv_mid, kv.at[2, 1], kv_ss.at[3], kv_rs.at[3], inner=relay_to)
    sideways = remote(kv.at[0], kv.at[3], kv_ss.at[4], kv_rs.at[4], outer=outer(1))
    forward = [one, values_mid, sideways, keys_two, values_two]
    for copy in forward[:3]:
        copy.start()

    def back(part, b):
        to = ({"inner": inner(-1)}, {"inner": inner(-2)}, {"outer": outer(-1)})[b - 1]
        at = (part, b - 1)
        return remote(gout.at[at], gin.at[at], g_ss.at[at], g_rs.at[at], **to)

    quarter = pl.ds(pl.multiple_of(c * (half_w // 2), half_w // 2), half_w // 2)
    w_remote = remote(
        weight.at[pl.ds(pl.multiple_of((1 - h) * half_w + c * (half_w // 2), half_w // 2), half_w // 2), :],
        w_oth.at[quarter, :],
        w_ss.at[0],
        w_rs.at[0],
        head=1 - h,
    )
    w_mate = remote(
        w_oth.at[quarter, :], w_oth.at[quarter, :], w_ss.at[1], w_rs.at[1], outer=core_mate
    )
    for by in range(1, N_Z):
        pl.semaphore_signal(ready, inc=1, device_id={"inner": at_z(by)}, device_id_type=MESH)
    w_local.start()
    for zz in range(N_Z):
        in_local(zz).start()
        in_remote(zz).start()

    mine = order[i * N_OUTER + o]
    block_ids = [None, inner(-1) * N_OUTER + o, inner(-2) * N_OUTER + o, i * N_OUTER + outer(-1)]
    bias = [None]
    for block_id in block_ids[1:]:
        bias.append(jnp.where(order[block_id] < mine, 0.0, FAR).astype(F32))

    def tile(t):
        return pl.ds(pl.multiple_of(t * TILE, TILE), TILE)

    def look_own():
        key = lax.broadcasted_iota(jnp.int32, (cut, TILE), 0)
        row = lax.broadcasted_iota(jnp.int32, (cut, TILE), 1)
        seen = key <= row // group
        for t in range(steps):
            cs = pl.ds(t * TILE, TILE)
            n = (t * cut) % tok + cut
            s = dot(kv[0, 0, :n, :], q[cs, :], NT)
            last = jnp.where(seen, s[n - cut :], FAR)
            s = last if n == cut else jnp.concatenate([s[: n - cut], last], axis=0)
            dp = dot(kv[0, 1, :n, :], go[cs, :], NT)
            here = jnp.max(s, axis=0, keepdims=True) * scale2
            e = jnp.exp2(s * scale2 - here)
            E[0, :n, cs] = e
            DP[0, :n, cs] = dp
            if n < tok:
                E[0, n:, cs] = jnp.zeros((tok - n, TILE), F32)
            top[0, :, cs] = here
            total[:, cs] = jnp.sum(e, axis=0, keepdims=True)
            delta[:, cs] = jnp.sum(e * dp, axis=0, keepdims=True)

    def look(b, before):
        def body(t, carry):
            cs = tile(t)
            s = dot(kv[b, 0], q[cs, :], NT)
            dp = dot(kv[b, 1], go[cs, :], NT)
            old = top[before, :, cs]
            new = jnp.maximum(old, jnp.max(s, axis=0, keepdims=True) * scale2 + bias[b])
            factor = jnp.exp2(old - new)
            e = jnp.exp2(s * scale2 - (new - bias[b]))
            E[b, :, cs] = e
            DP[b, :, cs] = dp
            top[b, :, cs] = new
            total[:, cs] = total[:, cs] * factor + jnp.sum(e, axis=0, keepdims=True)
            delta[:, cs] = delta[:, cs] * factor + jnp.sum(e * dp, axis=0, keepdims=True)
            return carry

        lax.fori_loop(0, steps, body, 0, unroll=6)

    def value_step(b, n, cs):
        p = (E[b, :n, cs] * fac[b, :, cs]).astype(BF16)
        return dot(p, go[cs, :], NN)

    def key_step(b, n, cs):
        ds = E[b, :n, cs] * fac[b, :, cs] * (DP[b, :n, cs] - delta[:, cs])
        E[b, :n, cs] = ds
        return dot(ds.astype(BF16), q[cs, :], NN)

    def block_sum(step, b):
        if b > 0:
            def body(t, total_so_far):
                return total_so_far + step(b, tok, tile(t))

            return lax.fori_loop(0, steps, body, jnp.zeros((tok, hd), F32), unroll=6)
        parts = [None] * (tok // cut)
        for t in range(steps):
            n = (t * cut) % tok + cut
            x = step(0, n, pl.ds(t * TILE, TILE))
            for k in range(n // cut):
                piece = x[k * cut : k * cut + cut]
                parts[k] = piece if parts[k] is None else parts[k] + piece
        return jnp.concatenate(parts, axis=0)

    q_in.wait()
    go_in.wait()
    look_own()
    keys_two.start()
    values_mid.wait_recv()
    values_two.start()
    sideways.wait_recv()
    w_remote.start()
    look(3, 0)
    one.wait_recv()
    look(1, 3)
    keys_two.wait_recv()
    values_two.wait_recv()
    look(2, 1)
    sums = total[...]
    delta[...] = delta[...] / sums
    lse = top[2] + jnp.log2(sums)
    for b in range(4):
        fac[b] = jnp.exp2(top[b] - lse)

    def to_core(part):
        at = (part, 0)
        return remote(pair.at[at], pair.at[part, 1], p_ss.at[at], p_rs.at[at], outer=core_mate)

    def to_head(part):
        at = (part, 1)
        return remote(pair.at[part, 0], pair.at[part, 2], p_ss.at[at], p_rs.at[at], head=1 - h)

    def send_back(part, b, grad):
        gout[part, b - 1] = grad.astype(BF16)
        back(part, b).start()

    def finish_pair(part, grad):
        for b in (2, 1, 3):
            back(part, b).wait_recv()
            grad = grad + gin[part, b - 1].astype(F32)
        pair[part, 0] = grad.astype(BF16)
        to_core(part).start()
        to_head(part).start()
        pair_t[part, :, :tok] = grad.T.astype(BF16)

    owner = y // 2 == c
    not_owner = y // 2 != c

    def z_at(zz):
        return lax.rem(z + 1 + zz, N_Z)

    def above(j):
        return lax.rem(y - (2 * c + j) + N_Y, N_Y)

    def y_copy(part, j, zz):
        return remote(
            ysend.at[part, j, zz],
            yrecv.at[part, above(j) - 1, zz],
            y_ss.at[part, j, zz],
            y_rs.at[part, above(j) - 1, zz],
            inner=at_y(2 * c + j),
        )

    def y_arrival(part, k, zz):
        return remote(
            ysend.at[part, 0, zz], yrecv.at[part, k, zz], y_ss.at[part, 0, zz],
            y_rs.at[part, k, zz], inner=at_y(lax.rem(y + 1, N_Y)),
        )

    def z_copy(part, zz, place):
        slot = 2 * zz + jnp.where(o // 2 == place // 2, 0, 1)
        return remote(
            zsend.at[part, zz, pl.ds(place * 32, 32), :],
            zrecv.at[part, slot],
            z_ss.at[part, zz, place],
            z_rs.at[part, slot],
            inner=z_at(zz) * N_Y + y,
            outer=place,
        )

    def z_arrival(part, slot):
        return remote(
            zsend.at[part, 0, pl.ds(0, 32), :], zrecv.at[part, slot], z_ss.at[part, 0, 0],
            z_rs.at[part, slot], inner=z_at(0) * N_Y + y,
        )

    def produce(part):
        to_core(part).wait_recv()
        pair_t[part, :, tok:] = pair[part, 1].astype(F32).T.astype(BF16)

        def body(zz, carry):
            x = dot(pair_t[part], inp[z_at(zz)], NN)
            for j in range(2):
                piece = x[:, j * hd : j * hd + hd]

                @pl.when(above(j) == 0)
                def _(piece=piece):
                    yacc[part, zz] = piece

                @pl.when(above(j) != 0)
                def _(piece=piece, j=j):
                    ysend[part, j, zz] = piece.astype(BF16)
                    y_copy(part, j, zz).start()

            return carry

        lax.fori_loop(0, N_Z, body, 0, unroll=2)

    def gather_y(part):
        @pl.when(owner)
        def _():
            def body(zz, carry):
                x = yacc[part, zz]
                for k in range(3):
                    y_arrival(part, k, zz).wait_recv()
                    x = x + yrecv[part, k, zz].astype(F32)
                x = x.T
                zsend[part, zz] = x.astype(BF16)
                for place in range(N_OUTER):

                    @pl.when((zz < N_Z - 1) | (place != o))
                    def _(place=place):
                        z_copy(part, zz, place).start()

                @pl.when(zz == N_Z - 1)
                def _():
                    for place in range(N_OUTER):

                        @pl.when(place == o)
                        def _(place=place):
                            zacc[part] = x[place * 32 : place * 32 + 32, :]

                return carry

            lax.fori_loop(0, N_Z, body, 0)

    def gather_z(part):
        @pl.when(not_owner)
        def _():
            z_arrival(part, 2 * N_Z - 2).wait_recv()
            zacc[part] = zrecv[part, 2 * N_Z - 2].astype(F32)

        def body(slot, x):
            z_arrival(part, slot).wait_recv()
            return x + zrecv[part, slot].astype(F32)

        x = lax.fori_loop(0, 2 * N_Z - 2, body, zacc[part])
        x = body(2 * N_Z - 1, x) / math.sqrt(tok * N_INNER * N_OUTER)
        wg[pl.ds(part, 32, 2), :] = x

    for b in (2, 1, 3):
        send_back(1, b, block_sum(value_step, b))
    values_own = block_sum(value_step, 0)
    send_back(0, 2, block_sum(key_step, 2) * scale)
    finish_pair(1, values_own)
    w_remote.wait_recv()
    w_mate.start()
    send_back(0, 1, block_sum(key_step, 1) * scale)
    for zz in range(N_Z):
        in_local(zz).wait()
        in_remote(zz).wait_recv()
    produce(1)
    send_back(0, 3, block_sum(key_step, 3) * scale)
    finish_pair(0, block_sum(key_step, 0) * scale)
    pl.semaphore_wait(ready, N_Z - 1)
    gather_y(1)
    produce(0)

    for b in range(4):
        k_t[:, b * tok : b * tok + tok] = kv[b, 0].astype(F32).T.astype(BF16)

    def finish_queries(t, carry):
        cs = tile(t)
        ds = E[:, :, cs].reshape(4 * tok, TILE).astype(BF16)
        dq[cs, :] = (dot(k_t[...], ds, NN) * scale).T.astype(BF16)
        return carry

    lax.fori_loop(0, steps, finish_queries, 0, unroll=3)
    dq_out.start()
    gather_y(0)
    w_local.wait()
    w_mate.wait_recv()
    for k, w in enumerate((w_own, w_oth)):
        w_cat[k, :, :hd] = w[pl.ds(0, half_d, 2), :]
        w_cat[k, :, hd:] = w[pl.ds(1, half_d, 2), :]
    to_head(1).wait_recv()
    to_head(0).wait_recv()

    def input_part(t, carry):
        cs = tile(t)
        term = jnp.zeros((tok, TILE), F32)
        for k, at in enumerate((0, 2)):
            both = jnp.concatenate([pair[0, at], pair[1, at]], axis=1)
            term = term + dot(both, w_cat[k, cs, :], NT)
        ig[:, cs] = term.astype(BF16)
        return carry

    lax.fori_loop(0, half_d // TILE, input_part, 0, unroll=4)
    ig_out.start()
    gather_z(1)
    gather_z(0)

    for copy in forward + [w_remote, w_mate]:
        copy.wait_send()
    for part in range(2):
        to_core(part).wait_send()
        to_head(part).wait_send()
        for b in (1, 2, 3):
            back(part, b).wait_send()

    def sent(zz, carry):
        in_remote(zz).wait_send()
        for part in range(2):
            for j in range(2):

                @pl.when(above(j) != 0)
                def _(part=part, j=j):
                    y_copy(part, j, zz).wait_send()

        return carry

    lax.fori_loop(0, N_Z, sent, 0)

    @pl.when(owner)
    def _():
        def sent_z(zz, carry):
            for part in range(2):
                for place in range(N_OUTER):

                    @pl.when((zz < N_Z - 1) | (place != o))
                    def _(part=part, place=place):
                        z_copy(part, zz, place).wait_send()

            return carry

        lax.fori_loop(0, N_Z, sent_z, 0)

    dq_out.wait()
    ig_out.wait()


def shards(queries, grad_out, keys_values, inputs, kv_weight, block_order):
    layers, tok, _, per_group, hd = queries.shape
    rows = layers * tok * per_group
    width = inputs.shape[1]
    vmem = pl.BlockSpec(memory_space=pltpu.VMEM)
    smem = pl.BlockSpec(memory_space=pltpu.SMEM)
    hbm = pl.BlockSpec(memory_space=pl.ANY)
    dma = pltpu.SemaphoreType.DMA
    scratch = [
        pltpu.VMEM((rows, hd), BF16),
        pltpu.VMEM((rows, hd), BF16),
        pltpu.VMEM((rows, hd), BF16),
        pltpu.VMEM((tok, width // 2), BF16),
        pltpu.VMEM((4, tok, rows), F32),
        pltpu.VMEM((4, tok, rows), F32),
        pltpu.VMEM((4, 1, rows), F32),
        pltpu.VMEM((1, rows), F32),
        pltpu.VMEM((1, rows), F32),
        pltpu.VMEM((4, 1, rows), F32),
        pltpu.VMEM((hd, 4 * tok), BF16),
        pltpu.VMEM((4, 2, tok, hd), BF16),
        pltpu.VMEM((tok, hd), BF16),
        pltpu.VMEM((2, 3, tok, hd), BF16),
        pltpu.VMEM((2, 3, tok, hd), BF16),
        pltpu.VMEM((N_Z, 2 * tok, 256), BF16),
        pltpu.VMEM((width, hd), BF16),
        pltpu.VMEM((width, hd), BF16),
        pltpu.VMEM((2, width // 2, 2 * hd), BF16),
        pltpu.VMEM((2, 3, tok, hd), BF16),
        pltpu.VMEM((2, hd, 2 * tok), BF16),
        pltpu.VMEM((2, 2, N_Z, hd, 128), BF16),
        pltpu.VMEM((2, 3, N_Z, hd, 128), BF16),
        pltpu.VMEM((2, N_Z, hd, 128), F32),
        pltpu.VMEM((2, N_Z, 128, hd), BF16),
        pltpu.VMEM((2, 2 * N_Z, 32, hd), BF16),
        pltpu.VMEM((2, 32, hd), F32),
        dma((5,)), dma((5,)), dma((2, 3)), dma((2, 3)),
        dma((N_Z,)), dma((N_Z,)), dma((N_Z,)), dma, dma((2,)), dma((2,)), dma((2, 2)), dma((2, 2)),
        dma((2, 2, N_Z)), dma((2, 3, N_Z)),
        dma((2, N_Z, N_OUTER)), dma((2, 2 * N_Z)), pltpu.SemaphoreType.REGULAR, dma((4,)),
    ]
    query_out, input_grad, weight_grad = pl.pallas_call(
        kernel,
        out_shape=[
            jax.ShapeDtypeStruct((rows, hd), BF16),
            jax.ShapeDtypeStruct((tok, width // 2), BF16),
            jax.ShapeDtypeStruct((64, hd), F32),
        ],
        in_specs=[hbm, hbm, vmem, smem, hbm, hbm],
        out_specs=[hbm, hbm, vmem],
        scratch_shapes=scratch,
        compiler_params=pltpu.CompilerParams(
            collective_id=0, has_side_effects=True, vmem_limit_bytes=60 * 2**20
        ),
        name="backward",
    )(
        queries.reshape(rows, hd),
        grad_out.reshape(rows, hd),
        keys_values.reshape(tok * 2, hd),
        block_order,
        inputs,
        kv_weight.reshape(width * 2, hd),
    )

    def handover(x, y, a, x_out, y_out, a_out, xs, ys, as_, r_sem, w_sem):
        parts = []
        for src, mid, dst, cuts in ((x, xs, x_out, 4), (y, ys, y_out, 4), (a, as_, a_out, 1)):
            n = src.shape[0] // cuts
            for k in range(cuts):
                at = pl.ds(k * n, n)
                parts.append((src.at[at, :], mid.at[at, :], dst.at[at, :]))
        reads = [pltpu.make_async_copy(s, m, r_sem.at[k]) for k, (s, m, _) in enumerate(parts)]
        writes = [pltpu.make_async_copy(m, d, w_sem.at[k]) for k, (_, m, d) in enumerate(parts)]
        for copy in reads:
            copy.start()
        for k, copy in enumerate(writes):
            reads[k].wait()
            copy.start()
        for copy in writes:
            copy.wait()

    query_out, input_grad, weight_grad = pl.pallas_call(
        handover,
        out_shape=[
            jax.ShapeDtypeStruct(query_out.shape, BF16),
            jax.ShapeDtypeStruct(input_grad.shape, BF16),
            jax.ShapeDtypeStruct((64, hd), F32),
        ],
        in_specs=[hbm, hbm, hbm],
        out_specs=[hbm, hbm, hbm],
        scratch_shapes=[
            pltpu.VMEM(query_out.shape, BF16),
            pltpu.VMEM(input_grad.shape, BF16),
            pltpu.VMEM((64, hd), F32),
            dma((9,)),
            dma((9,)),
        ],
        compiler_params=pltpu.CompilerParams(vmem_limit_bytes=60 * 2**20),
        name="handover",
    )(query_out, input_grad, weight_grad)

    return (
        query_out.reshape(queries.shape),
        input_grad,
        weight_grad.reshape(32, 1, 2, hd),
    )


def solution(mesh):
    return jax.shard_map(
        shards,
        mesh=mesh,
        in_specs=(
            P(None, ("inner", "outer"), "head", None, None),
            P(None, ("inner", "outer"), "head", None, None),
            P(("inner", "outer"), "head", None, None),
            P(("inner", "outer"), None),
            P(None, "head", None, None),
            P(),
        ),
        out_specs=(
            P(None, ("inner", "outer"), "head", None, None),
            P(("inner", "outer"), "head"),
            P(("inner", "outer"), "head", None, None),
        ),
        check_vma=False,
    )
```

```python
import functools
import math

import jax
import jax.numpy as jnp
from jax import lax
from jax.experimental import pallas as pl
from jax.experimental.pallas import tpu as pltpu
from jax.sharding import PartitionSpec as P

F32 = jnp.float32
BF16 = jnp.bfloat16
MESH = pl.DeviceIdType.MESH
N_INNER = 32
N_Y = 4
N_Z = 8
N_OUTER = 4
NT = (((1,), (1,)), ((), ()))
NN = (((1,), (0,)), ((), ()))
FAR = -1e30
TILE = 512


def dot(a, b, dims):
    return lax.dot_general(a, b, dims, preferred_element_type=F32)


def remote(src, dst, send, recv, **where):
    return pltpu.make_async_remote_copy(
        src_ref=src,
        dst_ref=dst,
        send_sem=send,
        recv_sem=recv,
        device_id=where,
        device_id_type=MESH,
    )


def kernel(
    q_hbm, go_hbm, kv_hbm, order, inputs, weight,
    dq_hbm, ig_hbm, wg,
    q, go, kv_raw, dq, ig,
    E, DP, top, total, delta, fac, k_t, kv, kv_mid, gout, gin, inp, w_own, w_oth, w_cat,
    pair, pair_t, ysend, yrecv, yacc, zsend, zrecv, zacc,
    kv_ss, kv_rs, g_ss, g_rs, in_ls, in_ss, in_rs, w_ls, w_ss, w_rs, p_ss, p_rs,
    y_ss, y_rs, z_ss, z_rs, ready, io_s,
):
    rows = q.shape[0]
    tok = kv.shape[2]
    hd = kv.shape[3]
    group = rows // 2 // tok
    scale = 1.0 / math.sqrt(hd)
    scale2 = scale * math.log2(math.e)
    half_w = w_own.shape[0]
    half_d = half_w // 2
    steps = rows // TILE
    cut = TILE // group
    i = lax.axis_index("inner")
    o = lax.axis_index("outer")
    h = lax.axis_index("head")
    z = i // N_Y
    y = lax.rem(i, N_Y)
    c = lax.rem(o, 2)

    def inner(by):
        return lax.rem(i + by + N_INNER, N_INNER)

    def outer(by):
        return lax.rem(o + by + N_OUTER, N_OUTER)

    def at_z(by):
        return lax.rem(z + by, N_Z) * N_Y + y

    def at_y(place):
        return z * N_Y + place

    core_mate = o + 1 - 2 * c
    relay_to = lax.rem(at_y(lax.rem(y + 1, N_Y)) + 2, N_INNER)
    two_back = inner(-2)
    relay_from = two_back // N_Y * N_Y + lax.rem(lax.rem(two_back, N_Y) + 3, N_Y)

    kv_in = pltpu.make_async_copy(kv_hbm, kv_raw, io_s.at[4])
    kv_in.start()
    barrier = pltpu.get_barrier_semaphore()
    greeted = [{"inner": inner(by)} for by in (1, 2, -1, -2)]
    greeted += [{"outer": outer(by)} for by in (1, 2, 3)]
    greeted += [{"head": 1 - h}, {"inner": relay_to}, {"inner": relay_from}]
    greeted += [{"inner": at_y(lax.rem(y + by, N_Y))} for by in (1, 2, 3)]
    greeted += [{"inner": at_z(by)} for by in range(1, N_Z)]
    for where in greeted:
        pl.semaphore_signal(barrier, inc=1, device_id=where, device_id_type=MESH)

    q_in = pltpu.make_async_copy(q_hbm, q, io_s.at[0])
    go_in = pltpu.make_async_copy(go_hbm, go, io_s.at[1])
    dq_out = pltpu.make_async_copy(dq, dq_hbm, io_s.at[2])
    ig_out = pltpu.make_async_copy(ig, ig_hbm, io_s.at[3])
    q_in.start()
    go_in.start()
    kv_in.wait()
    kv[0, 0] = kv_raw[pl.ds(0, tok, 2), :]
    kv[0, 1] = kv_raw[pl.ds(1, tok, 2), :]
    w_local = pltpu.make_async_copy(
        weight.at[pl.ds(pl.multiple_of(h * half_w, half_w), half_w), :], w_own, w_ls
    )

    def in_local(zz):
        return pltpu.make_async_copy(
            inputs.at[:, pl.ds(pl.multiple_of(zz * 512 + c * 256, 256), 256)],
            inp.at[zz, pl.ds(0, tok), :],
            in_ls.at[zz],
        )

    def in_remote(zz):
        return remote(
            inputs.at[:, pl.ds(pl.multiple_of(zz * 512 + (1 - c) * 256, 256), 256)],
            inp.at[zz, pl.ds(tok, tok), :],
            in_ss.at[zz],
            in_rs.at[zz],
            outer=core_mate,
        )

    pl.semaphore_wait(barrier, len(greeted))

    one = remote(kv.at[0], kv.at[1], kv_ss.at[0], kv_rs.at[0], inner=inner(1))
    keys_two = remote(kv.at[0, 0], kv.at[2, 0], kv_ss.at[1], kv_rs.at[1], inner=inner(2))
    values_mid = remote(
        kv.at[0, 1], kv_mid, kv_ss.at[2], kv_rs.at[2], inner=at_y(lax.rem(y + 3, N_Y))
    )
    values_two = remote(kv_mid, kv.at[2, 1], kv_ss.at[3], kv_rs.at[3], inner=relay_to)
    sideways = remote(kv.at[0], kv.at[3], kv_ss.at[4], kv_rs.at[4], outer=outer(1))
    forward = [one, values_mid, sideways, keys_two, values_two]
    for copy in forward[:3]:
        copy.start()

    def back(part, b):
        to = ({"inner": inner(-1)}, {"inner": inner(-2)}, {"outer": outer(-1)})[b - 1]
        at = (part, b - 1)
        return remote(gout.at[at], gin.at[at], g_ss.at[at], g_rs.at[at], **to)

    quarter = pl.ds(pl.multiple_of(c * (half_w // 2), half_w // 2), half_w // 2)
    w_remote = remote(
        weight.at[pl.ds(pl.multiple_of((1 - h) * half_w + c * (half_w // 2), half_w // 2), half_w // 2), :],
        w_oth.at[quarter, :],
        w_ss.at[0],
        w_rs.at[0],
        head=1 - h,
    )
    w_mate = remote(
        w_oth.at[quarter, :], w_oth.at[quarter, :], w_ss.at[1], w_rs.at[1], outer=core_mate
    )
    for by in range(1, N_Z):
        pl.semaphore_signal(ready, inc=1, device_id={"inner": at_z(by)}, device_id_type=MESH)
    w_local.start()
    for zz in range(N_Z):
        in_local(zz).start()
        in_remote(zz).start()

    mine = order[i * N_OUTER + o]
    block_ids = [None, inner(-1) * N_OUTER + o, inner(-2) * N_OUTER + o, i * N_OUTER + outer(-1)]
    bias = [None]
    for block_id in block_ids[1:]:
        bias.append(jnp.where(order[block_id] < mine, 0.0, FAR).astype(F32))

    def tile(t):
        return pl.ds(pl.multiple_of(t * TILE, TILE), TILE)

    def look_own():
        key = lax.broadcasted_iota(jnp.int32, (cut, TILE), 0)
        row = lax.broadcasted_iota(jnp.int32, (cut, TILE), 1)
        seen = key <= row // group
        for t in range(steps):
            cs = pl.ds(t * TILE, TILE)
            n = (t * cut) % tok + cut
            s = dot(kv[0, 0, :n, :], q[cs, :], NT)
            last = jnp.where(seen, s[n - cut :], FAR)
            s = last if n == cut else jnp.concatenate([s[: n - cut], last], axis=0)
            dp = dot(kv[0, 1, :n, :], go[cs, :], NT)
            here = jnp.max(s, axis=0, keepdims=True) * scale2
            e = jnp.exp2(s * scale2 - here)
            E[0, :n, cs] = e
            DP[0, :n, cs] = dp
            if n < tok:
                E[0, n:, cs] = jnp.zeros((tok - n, TILE), F32)
            top[0, :, cs] = here
            total[:, cs] = jnp.sum(e, axis=0, keepdims=True)
            delta[:, cs] = jnp.sum(e * dp, axis=0, keepdims=True)

    def look(b, before):
        def body(t, carry):
            cs = tile(t)
            s = dot(kv[b, 0], q[cs, :], NT)
            dp = dot(kv[b, 1], go[cs, :], NT)
            old = top[before, :, cs]
            new = jnp.maximum(old, jnp.max(s, axis=0, keepdims=True) * scale2 + bias[b])
            factor = jnp.exp2(old - new)
            e = jnp.exp2(s * scale2 - (new - bias[b]))
            E[b, :, cs] = e
            DP[b, :, cs] = dp
            top[b, :, cs] = new
            total[:, cs] = total[:, cs] * factor + jnp.sum(e, axis=0, keepdims=True)
            delta[:, cs] = delta[:, cs] * factor + jnp.sum(e * dp, axis=0, keepdims=True)
            return carry

        lax.fori_loop(0, steps, body, 0, unroll=6)

    def value_step(b, n, cs):
        p = (E[b, :n, cs] * fac[b, :, cs]).astype(BF16)
        return dot(p, go[cs, :], NN)

    def key_step(b, n, cs):
        ds = E[b, :n, cs] * fac[b, :, cs] * (DP[b, :n, cs] - delta[:, cs])
        E[b, :n, cs] = ds
        return dot(ds.astype(BF16), q[cs, :], NN)

    def block_sum(step, b):
        if b > 0:
            def body(t, total_so_far):
                return total_so_far + step(b, tok, tile(t))

            return lax.fori_loop(0, steps, body, jnp.zeros((tok, hd), F32), unroll=6)
        parts = [None] * (tok // cut)
        for t in range(steps):
            n = (t * cut) % tok + cut
            x = step(0, n, pl.ds(t * TILE, TILE))
            for k in range(n // cut):
                piece = x[k * cut : k * cut + cut]
                parts[k] = piece if parts[k] is None else parts[k] + piece
        return jnp.concatenate(parts, axis=0)

    q_in.wait()
    go_in.wait()
    look_own()
    keys_two.start()
    values_mid.wait_recv()
    values_two.start()
    sideways.wait_recv()
    w_remote.start()
    look(3, 0)
    one.wait_recv()
    look(1, 3)
    keys_two.wait_recv()
    values_two.wait_recv()
    look(2, 1)
    sums = total[...]
    delta[...] = delta[...] / sums
    lse = top[2] + jnp.log2(sums)
    for b in range(4):
        fac[b] = jnp.exp2(top[b] - lse)

    def to_core(part):
        at = (part, 0)
        return remote(pair.at[at], pair.at[part, 1], p_ss.at[at], p_rs.at[at], outer=core_mate)

    def to_head(part):
        at = (part, 1)
        return remote(pair.at[part, 0], pair.at[part, 2], p_ss.at[at], p_rs.at[at], head=1 - h)

    def send_back(part, b, grad):
        gout[part, b - 1] = grad.astype(BF16)
        back(part, b).start()

    def finish_pair(part, grad):
        for b in (2, 1, 3):
            back(part, b).wait_recv()
            grad = grad + gin[part, b - 1].astype(F32)
        pair[part, 0] = grad.astype(BF16)
        to_core(part).start()
        to_head(part).start()
        pair_t[part, :, :tok] = grad.T.astype(BF16)

    owner = y // 2 == c
    not_owner = y // 2 != c

    def z_at(zz):
        return lax.rem(z + 1 + zz, N_Z)

    def above(j):
        return lax.rem(y - (2 * c + j) + N_Y, N_Y)

    def y_copy(part, j, zz):
        return remote(
            ysend.at[part, j, zz],
            yrecv.at[part, above(j) - 1, zz],
            y_ss.at[part, j, zz],
            y_rs.at[part, above(j) - 1, zz],
            inner=at_y(2 * c + j),
        )

    def y_arrival(part, k, zz):
        return remote(
            ysend.at[part, 0, zz], yrecv.at[part, k, zz], y_ss.at[part, 0, zz],
            y_rs.at[part, k, zz], inner=at_y(lax.rem(y + 1, N_Y)),
        )

    def z_copy(part, zz, place):
        slot = 2 * zz + jnp.where(o // 2 == place // 2, 0, 1)
        return remote(
            zsend.at[part, zz, pl.ds(place * 32, 32), :],
            zrecv.at[part, slot],
            z_ss.at[part, zz, place],
            z_rs.at[part, slot],
            inner=z_at(zz) * N_Y + y,
            outer=place,
        )

    def z_arrival(part, slot):
        return remote(
            zsend.at[part, 0, pl.ds(0, 32), :], zrecv.at[part, slot], z_ss.at[part, 0, 0],
            z_rs.at[part, slot], inner=z_at(0) * N_Y + y,
        )

    def produce(part):
        to_core(part).wait_recv()
        pair_t[part, :, tok:] = pair[part, 1].astype(F32).T.astype(BF16)

        def body(zz, carry):
            x = dot(pair_t[part], inp[z_at(zz)], NN)
            for j in range(2):
                piece = x[:, j * hd : j * hd + hd]

                @pl.when(above(j) == 0)
                def _(piece=piece):
                    yacc[part, zz] = piece

                @pl.when(above(j) != 0)
                def _(piece=piece, j=j):
                    ysend[part, j, zz] = piece.astype(BF16)
                    y_copy(part, j, zz).start()

            return carry

        lax.fori_loop(0, N_Z, body, 0, unroll=2)

    def gather_y(part):
        @pl.when(owner)
        def _():
            def body(zz, carry):
                x = yacc[part, zz]
                for k in range(3):
                    y_arrival(part, k, zz).wait_recv()
                    x = x + yrecv[part, k, zz].astype(F32)
                x = x.T
                zsend[part, zz] = x.astype(BF16)
                for place in range(N_OUTER):

                    @pl.when((zz < N_Z - 1) | (place != o))
                    def _(place=place):
                        z_copy(part, zz, place).start()

                @pl.when(zz == N_Z - 1)
                def _():
                    for place in range(N_OUTER):

                        @pl.when(place == o)
                        def _(place=place):
                            zacc[part] = x[place * 32 : place * 32 + 32, :]

                return carry

            lax.fori_loop(0, N_Z, body, 0)

    def gather_z(part):
        @pl.when(not_owner)
        def _():
            z_arrival(part, 2 * N_Z - 2).wait_recv()
            zacc[part] = zrecv[part, 2 * N_Z - 2].astype(F32)

        def body(slot, x):
            z_arrival(part, slot).wait_recv()
            return x + zrecv[part, slot].astype(F32)

        x = lax.fori_loop(0, 2 * N_Z - 2, body, zacc[part])
        x = body(2 * N_Z - 1, x) / math.sqrt(tok * N_INNER * N_OUTER)
        wg[pl.ds(part, 32, 2), :] = x

    for b in (2, 1, 3):
        send_back(1, b, block_sum(value_step, b))
    values_own = block_sum(value_step, 0)
    send_back(0, 2, block_sum(key_step, 2) * scale)
    finish_pair(1, values_own)
    w_remote.wait_recv()
    w_mate.start()
    send_back(0, 1, block_sum(key_step, 1) * scale)
    for zz in range(N_Z):
        in_local(zz).wait()
        in_remote(zz).wait_recv()
    produce(1)
    send_back(0, 3, block_sum(key_step, 3) * scale)
    finish_pair(0, block_sum(key_step, 0) * scale)
    pl.semaphore_wait(ready, N_Z - 1)
    produce(0)
    gather_y(1)

    for b in range(4):
        k_t[:, b * tok : b * tok + tok] = kv[b, 0].astype(F32).T.astype(BF16)

    def finish_queries(t, carry):
        cs = tile(t)
        ds = E[:, :, cs].reshape(4 * tok, TILE).astype(BF16)
        dq[cs, :] = (dot(k_t[...], ds, NN) * scale).T.astype(BF16)
        return carry

    lax.fori_loop(0, steps, finish_queries, 0, unroll=3)
    dq_out.start()
    gather_y(0)
    w_local.wait()
    w_mate.wait_recv()
    for k, w in enumerate((w_own, w_oth)):
        w_cat[k, :, :hd] = w[pl.ds(0, half_d, 2), :]
        w_cat[k, :, hd:] = w[pl.ds(1, half_d, 2), :]
    to_head(1).wait_recv()
    to_head(0).wait_recv()

    def input_part(t, carry):
        cs = tile(t)
        term = jnp.zeros((tok, TILE), F32)
        for k, at in enumerate((0, 2)):
            both = jnp.concatenate([pair[0, at], pair[1, at]], axis=1)
            term = term + dot(both, w_cat[k, cs, :], NT)
        ig[:, cs] = term.astype(BF16)
        return carry

    lax.fori_loop(0, half_d // TILE, input_part, 0, unroll=4)
    ig_out.start()
    gather_z(1)
    gather_z(0)

    for copy in forward + [w_remote, w_mate]:
        copy.wait_send()
    for part in range(2):
        to_core(part).wait_send()
        to_head(part).wait_send()
        for b in (1, 2, 3):
            back(part, b).wait_send()

    def sent(zz, carry):
        in_remote(zz).wait_send()
        for part in range(2):
            for j in range(2):

                @pl.when(above(j) != 0)
                def _(part=part, j=j):
                    y_copy(part, j, zz).wait_send()

        return carry

    lax.fori_loop(0, N_Z, sent, 0)

    @pl.when(owner)
    def _():
        def sent_z(zz, carry):
            for part in range(2):
                for place in range(N_OUTER):

                    @pl.when((zz < N_Z - 1) | (place != o))
                    def _(part=part, place=place):
                        z_copy(part, zz, place).wait_send()

            return carry

        lax.fori_loop(0, N_Z, sent_z, 0)

    dq_out.wait()
    ig_out.wait()


def shards(queries, grad_out, keys_values, inputs, kv_weight, block_order):
    layers, tok, _, per_group, hd = queries.shape
    rows = layers * tok * per_group
    width = inputs.shape[1]
    vmem = pl.BlockSpec(memory_space=pltpu.VMEM)
    smem = pl.BlockSpec(memory_space=pltpu.SMEM)
    hbm = pl.BlockSpec(memory_space=pl.ANY)
    dma = pltpu.SemaphoreType.DMA
    scratch = [
        pltpu.VMEM((rows, hd), BF16),
        pltpu.VMEM((rows, hd), BF16),
        pltpu.VMEM((2 * tok, hd), BF16),
        pltpu.VMEM((rows, hd), BF16),
        pltpu.VMEM((tok, width // 2), BF16),
        pltpu.VMEM((4, tok, rows), F32),
        pltpu.VMEM((4, tok, rows), F32),
        pltpu.VMEM((4, 1, rows), F32),
        pltpu.VMEM((1, rows), F32),
        pltpu.VMEM((1, rows), F32),
        pltpu.VMEM((4, 1, rows), F32),
        pltpu.VMEM((hd, 4 * tok), BF16),
        pltpu.VMEM((4, 2, tok, hd), BF16),
        pltpu.VMEM((tok, hd), BF16),
        pltpu.VMEM((2, 3, tok, hd), BF16),
        pltpu.VMEM((2, 3, tok, hd), BF16),
        pltpu.VMEM((N_Z, 2 * tok, 256), BF16),
        pltpu.VMEM((width, hd), BF16),
        pltpu.VMEM((width, hd), BF16),
        pltpu.VMEM((2, width // 2, 2 * hd), BF16),
        pltpu.VMEM((2, 3, tok, hd), BF16),
        pltpu.VMEM((2, hd, 2 * tok), BF16),
        pltpu.VMEM((2, 2, N_Z, hd, 128), BF16),
        pltpu.VMEM((2, 3, N_Z, hd, 128), BF16),
        pltpu.VMEM((2, N_Z, hd, 128), F32),
        pltpu.VMEM((2, N_Z, 128, hd), BF16),
        pltpu.VMEM((2, 2 * N_Z, 32, hd), BF16),
        pltpu.VMEM((2, 32, hd), F32),
        dma((5,)), dma((5,)), dma((2, 3)), dma((2, 3)),
        dma((N_Z,)), dma((N_Z,)), dma((N_Z,)), dma, dma((2,)), dma((2,)), dma((2, 2)), dma((2, 2)),
        dma((2, 2, N_Z)), dma((2, 3, N_Z)),
        dma((2, N_Z, N_OUTER)), dma((2, 2 * N_Z)), pltpu.SemaphoreType.REGULAR, dma((5,)),
    ]
    query_out, input_grad, weight_grad = pl.pallas_call(
        kernel,
        out_shape=[
            jax.ShapeDtypeStruct((rows, hd), BF16),
            jax.ShapeDtypeStruct((tok, width // 2), BF16),
            jax.ShapeDtypeStruct((64, hd), F32),
        ],
        in_specs=[hbm, hbm, hbm, smem, hbm, hbm],
        out_specs=[hbm, hbm, vmem],
        scratch_shapes=scratch,
        compiler_params=pltpu.CompilerParams(
            collective_id=0, has_side_effects=True, vmem_limit_bytes=60 * 2**20
        ),
        name="backward",
    )(
        queries.reshape(rows, hd),
        grad_out.reshape(rows, hd),
        keys_values.reshape(tok * 2, hd),
        block_order,
        inputs,
        kv_weight.reshape(width * 2, hd),
    )

    def handover(x, y, a, x_out, y_out, a_out, xs, ys, as_, r_sem, w_sem):
        parts = []
        for src, mid, dst, cuts in ((x, xs, x_out, 4), (y, ys, y_out, 4), (a, as_, a_out, 1)):
            n = src.shape[0] // cuts
            for k in range(cuts):
                at = pl.ds(k * n, n)
                parts.append((src.at[at, :], mid.at[at, :], dst.at[at, :]))
        reads = [pltpu.make_async_copy(s, m, r_sem.at[k]) for k, (s, m, _) in enumerate(parts)]
        writes = [pltpu.make_async_copy(m, d, w_sem.at[k]) for k, (_, m, d) in enumerate(parts)]
        for copy in reads:
            copy.start()
        for k, copy in enumerate(writes):
            reads[k].wait()
            copy.start()
        for copy in writes:
            copy.wait()

    query_out, input_grad, weight_grad = pl.pallas_call(
        handover,
        out_shape=[
            jax.ShapeDtypeStruct(query_out.shape, BF16),
            jax.ShapeDtypeStruct(input_grad.shape, BF16),
            jax.ShapeDtypeStruct((64, hd), F32),
        ],
        in_specs=[hbm, hbm, hbm],
        out_specs=[hbm, hbm, hbm],
        scratch_shapes=[
            pltpu.VMEM(query_out.shape, BF16),
            pltpu.VMEM(input_grad.shape, BF16),
            pltpu.VMEM((64, hd), F32),
            dma((9,)),
            dma((9,)),
        ],
        compiler_params=pltpu.CompilerParams(vmem_limit_bytes=60 * 2**20),
        name="handover",
    )(query_out, input_grad, weight_grad)

    return (
        query_out.reshape(queries.shape),
        input_grad,
        weight_grad.reshape(32, 1, 2, hd),
    )


def solution(mesh):
    return jax.shard_map(
        shards,
        mesh=mesh,
        in_specs=(
            P(None, ("inner", "outer"), "head", None, None),
            P(None, ("inner", "outer"), "head", None, None),
            P(("inner", "outer"), "head", None, None),
            P(("inner", "outer"), None),
            P(None, "head", None, None),
            P(),
        ),
        out_specs=(
            P(None, ("inner", "outer"), "head", None, None),
            P(("inner", "outer"), "head"),
            P(("inner", "outer"), "head", None, None),
        ),
        check_vma=False,
    )
```
